256 devices in a mesh: blk: 16 (over y, z_lo, core), win: 16 (over x, z_hi).
Axes of the slice: x: 4, y: 4, z: 8 (z_hi: 4, z_lo: 2; z = z_hi * 2 + z_lo), core: 2. Of those that a mesh axis runs over, the one named last changes fastest.
Arguments:
- spectra: float32 [2, 64, 192, 4096], P(None, 'win', None, 'blk'), may hold values from -6 to 6
- masks: int32 [64, 4096], P('win', 'blk'), may hold values 0 or 1
- plan: int32 [2, 16], replicated, may hold values from 0 to 15, as said below
Outputs:
- correlations: float32 [2, 4096, 32, 256], P(None, ('blk', 'win'))
The draws below stay inside these ranges and needn't reach their ends.
Inputs may be any that keep to these rules, and one draw needn't show every extreme that they name: `plan`: in round r every block b has partner b XOR m_r for one nonzero m_r of that round; the m_r differ between rounds.
All inputs are finite; a program needn't handle non-finite values. No bound on the sum of `masks` on one device may be relied on, other than what follows from the above.
Results may differ from the reference program's by a relative error of at most 0.0003.
Values sent between devices are 32-bit elements; how exact they have to be, the bound alone decides.
No kernel may reach another device: no remote copies, remote signals or barrier semaphores. Data moves between devices by JAX's collectives and lax.ppermute only.
A program may use at most 128 MiB of HBM per device.

```python
import math
import jax
import jax.numpy as jnp
from jax import lax

CH_BLK = 256
F = 192
LAGS = 32
ROUNDS = 2
WINDOWS = 64
CHANNELS = 4096
N_BLK = 16


def draw_plan(key, part):
    key = jax.random.fold_in(key, 7)
    offsets = jax.random.permutation(key, N_BLK - 1) + 1
    chosen = offsets[:ROUNDS]
    blocks = jnp.arange(N_BLK, dtype=jnp.int32)
    return jnp.bitwise_xor(blocks[None, :], chosen[:, None].astype(jnp.int32)).astype(jnp.int32)


def with_ends(result, key, smallest, top_value):
    place = [jax.random.randint(jax.random.fold_in(key, axis), (), 0, length) for axis, length in enumerate(result.shape)]
    main_axis = result.shape.index(max(result.shape))
    next_to = place[:main_axis] + [(place[main_axis] + 1) % result.shape[main_axis]] + place[main_axis + 1:]
    return result.at[tuple(place)].set(smallest).at[tuple(next_to)].set(top_value)


def steps_of(stream_key, shape, split, low, largest):
    level, own = 1.0, jax.random.fold_in(stream_key, 6)
    for position, parts in split:
        draws = jnp.exp(jax.random.uniform(jax.random.fold_in(own, position), (parts,), jnp.float32, low / len(split), largest / len(split)))
        level = level * jnp.repeat(draws, shape[position] // parts).reshape([-1 if axis == position else 1 for axis in range(len(shape))])
    return level


def centred(own_key, shape, width, reach, pieces=(), kind=jnp.bfloat16):
    drawn = width * jax.random.normal(own_key, shape, jnp.float32)
    if pieces:
        drawn = drawn * steps_of(own_key, shape, pieces, -0.22, 0.18)
    return jnp.clip(drawn, -reach, reach).astype(kind)


def setup_inputs(seed: int = 0) -> dict:
    splits = jax.random.split(jax.random.key(seed), 4)
    return {
        "spectra": centred(splits[0], (2, WINDOWS, F, CHANNELS), 1.0, 6.0, ((1, 16), (3, 16)), jnp.float32),
        "masks": with_ends((jax.random.randint(splits[1], (WINDOWS, CHANNELS), 0, 4) < 3).astype(jnp.int32), jax.random.fold_in(splits[1], 1), 0, 1),
        "plan": draw_plan(jax.random.fold_in(splits[3], 71), 0),
    }


def whiten(spectra, masks):
    power = lax.optimization_barrier(jnp.mean(spectra[0] * spectra[0] + spectra[1] * spectra[1], axis=1, keepdims=True))
    scale = masks[:, None, :].astype(jnp.float32) * lax.rsqrt(power + 1e-06)
    return spectra * scale[None]

def lag_tables():
    shift = (jnp.arange(LAGS) - LAGS // 2).astype(jnp.float32)
    freq = jnp.arange(F).astype(jnp.float32)
    angle = math.pi * shift[:, None] * freq[None, :] / F
    return (jnp.cos(angle), jnp.sin(angle))

def reference(spectra, masks, plan):
    white = whiten(spectra, masks)
    cos_t, sin_t = lag_tables()
    norm = 1.0 / math.sqrt(WINDOWS * F)
    high = lax.Precision.HIGHEST
    outputs = []
    for r in range(ROUNDS):

        def one_block(b):
            p = plan[r, b]
            own = lax.dynamic_slice_in_dim(white, (b * CH_BLK).astype(jnp.int32), CH_BLK, 3)
            other = lax.dynamic_slice_in_dim(white, (p * CH_BLK).astype(jnp.int32), CH_BLK, 3)
            real = jnp.einsum('wfi,wfj->fij', own[0], other[0], precision=high) + jnp.einsum('wfi,wfj->fij', own[1], other[1], precision=high)
            imag = jnp.einsum('wfi,wfj->fij', own[0], other[1], precision=high) - jnp.einsum('wfi,wfj->fij', own[1], other[0], precision=high)
            lagged = jnp.einsum('lf,fij->ilj', cos_t, real, precision=high) - jnp.einsum('lf,fij->ilj', sin_t, imag, precision=high)
            return lagged * norm
        blocks = lax.map(one_block, jnp.arange(N_BLK, dtype=jnp.int32))
        outputs.append(blocks.reshape(CHANNELS, LAGS, CH_BLK))
    return jnp.stack(outputs, axis=0)
```

```python
import functools
import math

import jax
import jax.numpy as jnp
import ml_dtypes
import numpy as np
from jax import lax
from jax.experimental import pallas as pl
from jax.experimental.pallas import tpu as pltpu
from jax.sharding import Mesh
from jax.sharding import PartitionSpec as P

LAGS = 32
BINS = 192
WINDOWS = 64
HALF = BINS // 2
STEP = 16
STEPS = HALF // STEP


def lag_table():
    tau = np.arange(LAGS) - LAGS // 2
    norm = 1.0 / math.sqrt(WINDOWS * BINS)
    bins = np.arange(BINS).reshape(2, STEPS, STEP).transpose(1, 2, 0)
    theta = np.pi * bins[..., None] * tau / BINS
    both = np.stack([np.cos(theta), -np.sin(theta)], axis=3) * norm
    table = np.einsum("sfhpl,jk->sjlfhpk", both, np.eye(8))
    table = table.reshape(STEPS, 8 * LAGS, STEP * 4 * 8).astype(np.float32)
    high = table.astype(ml_dtypes.bfloat16)
    low = (table - high.astype(np.float32)).astype(ml_dtypes.bfloat16)
    return high, low


def halves(value):
    high = value.astype(jnp.bfloat16)
    return high, (value - high.astype(jnp.float32)).astype(jnp.bfloat16)


def whiten_kernel(spectra_ref, masks_ref, own_ref, rows_ref):
    parts, windows, bins, channels = spectra_ref.shape
    pieces = []
    scales = []
    for w in range(windows):
        a, b = spectra_ref[0, w], spectra_ref[1, w]
        power = jnp.sum(a * a + b * b, axis=0, keepdims=True) * (1.0 / bins)
        scales.append(masks_ref[w : w + 1, :].astype(jnp.float32) * lax.rsqrt(power + 1e-06))
    for p in range(parts):
        for w in range(windows):
            pieces.append(spectra_ref[p, w] * scales[w])
    white = jnp.swapaxes(jnp.stack(pieces, axis=0), 0, 1)
    own_ref[...] = white
    lane = lax.broadcasted_iota(jnp.int32, (HALF, 8, 128), 2)
    for block in range(channels // 128):
        a = white[:HALF, :, block * 128 : (block + 1) * 128]
        b = white[HALF:, :, block * 128 : (block + 1) * 128]
        rows_ref[2 * block] = jnp.where(lane < 64, a, pltpu.roll(b, 64, axis=2))
        rows_ref[2 * block + 1] = jnp.where(lane < 64, pltpu.roll(a, 64, axis=2), b)


def whiten(spectra, masks):
    return pl.pallas_call(
        whiten_kernel,
        out_shape=(
            jax.ShapeDtypeStruct((BINS, 8, 256), jnp.float32),
            jax.ShapeDtypeStruct((4, HALF, 8, 128), jnp.float32),
        ),
        compiler_params=pltpu.CompilerParams(vmem_limit_bytes=32 * 2**20),
        name="whiten",
    )(spectra, masks)


def stack_kernel(rows_ref, own_ref, high_ref, low_ref, out_ref, prod_ref):
    step = pl.program_id(0)
    sign = jnp.where(lax.broadcasted_iota(jnp.int32, (4, 8, 128), 1) < 4, -1.0, 1.0)

    def one_low(f, _):
        p = rows_ref[:, f]
        q = pltpu.roll(p, 4, axis=1) * sign
        left = jnp.concatenate([p.reshape(32, 128), q.reshape(32, 128)], axis=1)
        lh, ll = halves(left)
        left = jnp.concatenate([lh, lh, ll], axis=0).T
        for h in range(2):
            right = own_ref[:, h, f].reshape(32, 256)
            rh, rl = halves(right)
            right = jnp.concatenate([rh, rl, rh], axis=0)
            rows = jnp.concatenate([left[64 * h : 64 * h + 64], left[128 + 64 * h : 192 + 64 * h]], axis=0)
            prod_ref[2 * f + h] = jnp.dot(rows, right, preferred_element_type=jnp.float32).reshape(2, 64, 256)
        return 0

    lax.fori_loop(0, STEP, one_low, 0, unroll=4)

    @pl.when(step == 0)
    def _():
        out_ref[...] = jnp.zeros_like(out_ref)

    gh, gl = high_ref[0], low_ref[0]
    for t in range(8):
        value = prod_ref[:, :, 8 * t : 8 * t + 8].reshape(STEP * 32, 256)
        vh, vl = halves(value)
        dot = functools.partial(jnp.dot, preferred_element_type=jnp.float32)
        lagged = dot(gh, vh) + dot(gl, vh) + dot(gh, vl)
        out_ref[8 * t : 8 * t + 8] += lagged.reshape(8, LAGS, 256)


def stack(rows, own, high, low):
    own = own.reshape(4, 2, HALF, 8, 256)
    return pl.pallas_call(
        stack_kernel,
        grid=(STEPS,),
        in_specs=[
            pl.BlockSpec((4, STEP, 8, 128), lambda s: (0, s, 0, 0)),
            pl.BlockSpec((4, 2, STEP, 8, 256), lambda s: (0, 0, s, 0, 0)),
            pl.BlockSpec((1, 8 * LAGS, STEP * 32), lambda s: (s, 0, 0)),
            pl.BlockSpec((1, 8 * LAGS, STEP * 32), lambda s: (s, 0, 0)),
        ],
        out_specs=pl.BlockSpec((64, LAGS, 256), lambda s: (0, 0, 0)),
        out_shape=jax.ShapeDtypeStruct((64, LAGS, 256), jnp.float32),
        scratch_shapes=[pltpu.VMEM((2 * STEP, 2, 64, 256), jnp.float32)],
        compiler_params=pltpu.CompilerParams(vmem_limit_bytes=40 * 2**20),
        cost_estimate=pl.CostEstimate(flops=16 * 10**9, bytes_accessed=14 * 2**20, transcendentals=0),
        name="stack",
    )(rows, own, high, low)


def to_partner(value, offset):
    count = lax.axis_size("blk")

    def by(mask):
        return lambda v: lax.ppermute(v, "blk", [(b, b ^ mask) for b in range(count)])

    return lax.switch(offset - 1, [by(mask) for mask in range(1, count)], value)


def on_device(spectra, masks, plan):
    high, low = (jnp.asarray(t) for t in lag_table())
    own, rows = whiten(spectra, masks)
    own = lax.all_gather(own, "x", axis=0, tiled=False)
    rows = lax.all_to_all(rows, "x", split_axis=0, concat_axis=0, tiled=True)
    rounds = plan.shape[0]
    theirs = [to_partner(rows, plan[r, 0]) for r in range(rounds)]
    partial = [stack(theirs[r], own, high, low) for r in range(rounds)]
    sums = [lax.psum_scatter(partial[r], "zh", scatter_dimension=0, tiled=True) for r in range(rounds)]
    return jnp.stack([to_partner(sums[r], plan[r, 0]) for r in range(rounds)], axis=0)


def solution(mesh):
    fine = Mesh(mesh.devices.reshape(16, 4, 4), ("blk", "x", "zh"))
    return jax.shard_map(
        on_device,
        mesh=fine,
        in_specs=(P(None, ("x", "zh"), None, "blk"), P(("x", "zh"), "blk"), P()),
        out_specs=P(None, ("blk", "x", "zh"), None, None),
        check_vma=False,
    )
```

```python
import functools
import math

import jax
import jax.numpy as jnp
import ml_dtypes
import numpy as np
from jax import lax
from jax.experimental import pallas as pl
from jax.experimental.pallas import tpu as pltpu
from jax.sharding import Mesh
from jax.sharding import PartitionSpec as P

LAGS = 32
BINS = 192
WINDOWS = 64
HALF = BINS // 2
STEP = 16
STEPS = HALF // STEP
EVEN = 18
ODD = 16
SMEM = pl.BlockSpec(memory_space=pltpu.SMEM)


def lag_tables():
    norm = 1.0 / math.sqrt(WINDOWS * BINS)
    bins = np.arange(BINS).reshape(2, STEPS, STEP).transpose(1, 2, 0)
    tables = []
    for turn, lags in ((np.cos, np.arange(EVEN)), (np.sin, np.arange(1, ODD + 1))):
        wave = turn(np.pi * bins[..., None] * lags / BINS) * norm * (lags <= LAGS // 2)
        table = np.einsum("sfhl,jk->sljfhk", wave, np.eye(8))
        table = table.reshape(STEPS, 8 * len(lags), STEP * 2 * 8).astype(np.float32)
        high = table.astype(ml_dtypes.bfloat16)
        low = (table - high.astype(np.float32)).astype(ml_dtypes.bfloat16)
        tables.append(np.concatenate([high, low], axis=1))
    return tables


def halves(value):
    high = value.astype(jnp.bfloat16)
    return high, (value - high.astype(jnp.float32)).astype(jnp.bfloat16)


def whiten_kernel(flag_ref, spectra_ref, masks_ref, own_ref, rows_ref):
    parts, windows, bins, channels = spectra_ref.shape
    pieces = []
    scales = []
    for w in range(windows):
        a, b = spectra_ref[0, w], spectra_ref[1, w]
        power = jnp.sum(a * a + b * b, axis=0, keepdims=True) * (1.0 / bins)
        scales.append(masks_ref[w : w + 1, :].astype(jnp.float32) * lax.rsqrt(power + 1e-06))
    for p in range(parts):
        for w in range(windows):
            pieces.append(spectra_ref[p, w] * scales[w])
    white = jnp.swapaxes(jnp.stack(pieces, axis=0), 0, 1)
    own_ref[...] = white
    lane = lax.broadcasted_iota(jnp.int32, (HALF, 8, 128), 2)
    other = 1 - flag_ref[0]
    for block in range(channels // 128):
        a = white[:HALF, :, block * 128 : (block + 1) * 128]
        b = white[HALF:, :, block * 128 : (block + 1) * 128]
        place = 2 * jnp.where(other == 1, 1 - block, block)
        rows_ref[place] = jnp.where(lane < 64, a, pltpu.roll(b, 64, axis=2))
        rows_ref[place + 1] = jnp.where(lane < 64, pltpu.roll(a, 64, axis=2), b)


def whiten(flag, spectra, masks):
    return pl.pallas_call(
        whiten_kernel,
        in_specs=[SMEM, pl.BlockSpec(memory_space=pltpu.VMEM), pl.BlockSpec(memory_space=pltpu.VMEM)],
        out_shape=(
            jax.ShapeDtypeStruct((BINS, 8, 256), jnp.float32),
            jax.ShapeDtypeStruct((4, HALF, 8, 128), jnp.float32),
        ),
        compiler_params=pltpu.CompilerParams(vmem_limit_bytes=32 * 2**20),
        name="whiten",
    )(flag, spectra, masks)


def stack_kernel(side_ref, rows_ref, own_ref, cos_ref, sin_ref, out_ref, prod_ref, even_ref, odd_ref):
    step = pl.program_id(0)
    sign = jnp.where(lax.broadcasted_iota(jnp.int32, (4, 8, 128), 1) < 4, -1.0, 1.0)
    dot = functools.partial(jnp.dot, preferred_element_type=jnp.float32)

    def one_low(f, _):
        p = rows_ref[:, f]
        q = pltpu.roll(p, 4, axis=1) * sign
        left = jnp.concatenate([p.reshape(32, 128), q.reshape(32, 128)], axis=1)
        lh, ll = halves(left)
        left = jnp.concatenate([lh, lh, ll], axis=0).T
        for h in range(2):
            rh, rl = halves(own_ref[:, h, f].reshape(32, 128))
            right = jnp.concatenate([rh, rl, rh], axis=0)
            rows = jnp.concatenate([left[64 * h : 64 * h + 64], left[128 + 64 * h : 192 + 64 * h]], axis=0)
            prod_ref[2 * f + h] = dot(rows, right).reshape(2, 64, 128)
        return 0

    lax.fori_loop(0, STEP, one_low, 0, unroll=4)

    @pl.when(step == 0)
    def _():
        even_ref[...] = jnp.zeros_like(even_ref)
        odd_ref[...] = jnp.zeros_like(odd_ref)

    for t in range(4):
        for part, table_ref, sum_ref in ((0, cos_ref, even_ref), (1, sin_ref, odd_ref)):
            size = sum_ref.shape[1]
            value = jnp.concatenate(
                [prod_ref[:, part, 8 * t : 8 * t + 8], prod_ref[:, part, 32 + 8 * t : 40 + 8 * t]], axis=2
            ).reshape(STEP * 16, 256)
            vh, vl = halves(value)
            both = dot(table_ref[0], vh)
            sum_ref[t] += both[:size] + both[size:] + dot(table_ref[0, :size], vl)

    @pl.when(step == STEPS - 1)
    def _():
        mid = LAGS // 2
        for t in range(4):
            even = even_ref[t].reshape(EVEN, 8, 256)
            odd = odd_ref[t].reshape(ODD, 8, 256)
            for k in range(2):
                tile = t + 4 * k
                place = pl.ds(8 * (tile % 2), 8)
                e, o = even[:, :, 128 * k : 128 * k + 128], odd[:, :, 128 * k : 128 * k + 128]
                out_ref[tile // 2, mid, place] = e[0]
                for lag in range(1, mid + 1):
                    out_ref[tile // 2, mid + lag, place] = e[lag] - o[lag - 1]
                    out_ref[tile // 2, mid - lag, place] = e[lag] + o[lag - 1]


def stack(side, rows, own, cos_t, sin_t):
    own = own.reshape(4, 2, HALF, 8, 256)
    return pl.pallas_call(
        stack_kernel,
        grid_spec=pltpu.PrefetchScalarGridSpec(
            num_scalar_prefetch=1,
            grid=(STEPS,),
            in_specs=[
                pl.BlockSpec((4, STEP, 8, 128), lambda s, side: (0, s, 0, 0)),
                pl.BlockSpec((4, 2, STEP, 8, 128), lambda s, side: (0, 0, s, 0, side[0])),
                pl.BlockSpec((1,) + cos_t.shape[1:], lambda s, side: (s, 0, 0)),
                pl.BlockSpec((1,) + sin_t.shape[1:], lambda s, side: (s, 0, 0)),
            ],
            out_specs=pl.BlockSpec((4, LAGS + 1, 16, 128), lambda s, side: (0, 0, 0, 0)),
            scratch_shapes=[
                pltpu.VMEM((2 * STEP, 2, 64, 128), jnp.float32),
                pltpu.VMEM((4, 8 * EVEN, 256), jnp.float32),
                pltpu.VMEM((4, 8 * ODD, 256), jnp.float32),
            ],
        ),
        out_shape=jax.ShapeDtypeStruct((4, LAGS + 1, 16, 128), jnp.float32),
        compiler_params=pltpu.CompilerParams(vmem_limit_bytes=32 * 2**20),
        cost_estimate=pl.CostEstimate(flops=8 * 10**9, bytes_accessed=8 * 2**20, transcendentals=0),
        name="stack",
    )(side, rows, own, cos_t, sin_t)


def pack_kernel(sums_ref, out_ref):
    block = lax.broadcasted_iota(jnp.int32, (16, 128), 1) // 16
    for g in range(4):
        found = [None] * 8
        for k in range(8):
            value = sums_ref[LAGS - 8 * g - k]
            for d in range(8):
                turned = value if d == k else pltpu.roll(value, 16 * ((k - d) % 8), axis=1)
                found[d] = turned if k == 0 else jnp.where(block == k, turned, found[d])
        for d in range(8):
            out_ref[d, g] = found[d]


def pack(sums):
    return pl.pallas_call(
        pack_kernel,
        out_shape=jax.ShapeDtypeStruct((8, 4, 16, 128), jnp.float32),
        name="pack",
    )(sums)


def finish_kernel(flags_ref, *refs):
    out_ref = refs[-1]
    rounds = out_ref.shape[0]
    for r in range(rounds):
        straight_ref, shifted_ref, turned_ref = refs[3 * r : 3 * r + 3]
        near = jnp.where(flags_ref[0] == 0, shifted_ref[:LAGS], straight_ref[:LAGS])
        far = jnp.concatenate(
            [turned_ref[:, g].reshape(128, 128).T.reshape(8, 16, 128) for g in range(4)], axis=0
        )
        first = flags_ref[1] == 0
        full = jnp.concatenate([jnp.where(first, far, near), jnp.where(first, near, far)], axis=2)
        out_ref[r] = jnp.swapaxes(full, 0, 1)


def finish(flags, pieces):
    rounds = len(pieces)
    flat = [array for piece in pieces for array in piece]
    return pl.pallas_call(
        finish_kernel,
        in_specs=[SMEM] + [pl.BlockSpec(memory_space=pltpu.VMEM)] * len(flat),
        out_shape=jax.ShapeDtypeStruct((rounds, 16, LAGS, 256), jnp.float32),
        name="finish",
    )(flags, *flat)


def by_offset(send, value, offset):
    count = lax.axis_size("blk")
    return lax.switch(offset - 1, [functools.partial(send, mask) for mask in range(1, count)], value)


def send_rows(mask, value):
    return lax.ppermute(value, "blk", [(b, b ^ mask) for b in range(lax.axis_size("blk"))])


def send_sums(mask, value):
    count = lax.axis_size("blk")
    pairs = [(2 * b + x, 2 * (b ^ mask) + (x ^ 1)) for b in range(count) for x in range(2)]
    return send_rows(mask, value), lax.ppermute(value, ("blk", "xh"), pairs)


def low_bit(value):
    return value & -value


def on_device(spectra, masks, plan):
    rounds = plan.shape[0]
    cos_t, sin_t = (jnp.asarray(t) for t in lag_tables())
    common = plan[0, 0] & plan[1, 0]
    chosen = jnp.where(common != 0, low_bit(common), low_bit(plan[0, 0]) | low_bit(plan[1, 0]))
    flag = lax.population_count(chosen & lax.axis_index("blk")) & 1
    side = lax.axis_index("xh")
    own, rows = whiten(flag[None], spectra, masks)
    own = lax.all_gather(own, ("xh", "xl"), axis=0, tiled=False)
    rows = lax.all_to_all(rows, ("xh", "xl"), split_axis=0, concat_axis=0, tiled=True)
    theirs = [by_offset(send_rows, rows, plan[r, 0]) for r in range(rounds)]
    partial = [stack(side[None], theirs[r], own, cos_t, sin_t) for r in range(rounds)]
    sums = [lax.psum_scatter(partial[r], "zh", scatter_dimension=0, tiled=True)[0] for r in range(rounds)]
    pieces = []
    for r in range(rounds):
        turned = lax.all_to_all(pack(sums[r]), ("xl", "zh"), split_axis=0, concat_axis=0, tiled=True)
        pieces.append((*by_offset(send_sums, sums[r], plan[r, 0]), turned))
    return finish(jnp.stack([flag, side ^ flag]), pieces)


def solution(mesh):
    fine = Mesh(mesh.devices.reshape(16, 2, 2, 4), ("blk", "xh", "xl", "zh"))
    return jax.shard_map(
        on_device,
        mesh=fine,
        in_specs=(P(None, ("xh", "xl", "zh"), None, "blk"), P(("xh", "xl", "zh"), "blk"), P()),
        out_specs=P(None, ("blk", "xh", "xl", "zh"), None, None),
        check_vma=False,
    )
```

```python
import functools
import math

import jax
import jax.numpy as jnp
import ml_dtypes
import numpy as np
from jax import lax
from jax.experimental import pallas as pl
from jax.experimental.pallas import tpu as pltpu
from jax.sharding import Mesh
from jax.sharding import PartitionSpec as P

LAGS = 32
BINS = 192
WINDOWS = 64
HALF = BINS // 2
STEP = 16
STEPS = HALF // STEP
EVEN = 18
ODD = 16
SMEM = pl.BlockSpec(memory_space=pltpu.SMEM)


def lag_tables():
    norm = 1.0 / math.sqrt(WINDOWS * BINS)
    bins = np.arange(BINS).reshape(2, STEPS, STEP).transpose(1, 2, 0)
    tables = []
    for turn, lags in ((np.cos, np.arange(EVEN)), (np.sin, np.arange(1, ODD + 1))):
        wave = turn(np.pi * bins[..., None] * lags / BINS) * norm * (lags <= LAGS // 2)
        table = np.einsum("sfhl,jk->sljfhk", wave, np.eye(8))
        table = table.reshape(STEPS, 8 * len(lags), STEP * 2 * 8).astype(np.float32)
        high = table.astype(ml_dtypes.bfloat16)
        low = (table - high.astype(np.float32)).astype(ml_dtypes.bfloat16)
        tables.append(np.concatenate([high, low], axis=1))
    return tables


def halves(value):
    high = value.astype(jnp.bfloat16)
    return high, (value - high.astype(jnp.float32)).astype(jnp.bfloat16)


def whiten_kernel(place_ref, spectra_ref, masks_ref, near_ref, far_ref, *rows_refs):
    parts, windows, bins, channels = spectra_ref.shape
    pieces = []
    scales = []
    for w in range(windows):
        a, b = spectra_ref[0, w], spectra_ref[1, w]
        power = jnp.sum(a * a + b * b, axis=0, keepdims=True) * (1.0 / bins)
        scales.append(masks_ref[w : w + 1, :].astype(jnp.float32) * lax.rsqrt(power + 1e-06))
    for p in range(parts):
        for w in range(windows):
            pieces.append(spectra_ref[p, w] * scales[w])
    white = jnp.swapaxes(jnp.stack(pieces, axis=0), 0, 1)
    lane = lax.broadcasted_iota(jnp.int32, (HALF, 8, 128), 2)

    for side in range(2):

        @pl.when(place_ref[0] == side)
        def _():
            near_ref[...] = white[:, :, side * 128 : side * 128 + 128]
            far_ref[...] = white[:, :, 128 - side * 128 : 256 - side * 128]

    quarters = []
    for block in range(channels // 128):
        a = white[:HALF, :, block * 128 : (block + 1) * 128]
        b = white[HALF:, :, block * 128 : (block + 1) * 128]
        quarters.append(jnp.where(lane < 64, a, pltpu.roll(b, 64, axis=2)))
        quarters.append(jnp.where(lane < 64, pltpu.roll(a, 64, axis=2), b))
    for own in range(4):

        @pl.when(place_ref[1] == own)
        def _():
            for quarter in range(4):
                rows_refs[quarter ^ own][...] = quarters[quarter]


def whiten(place, spectra, masks):
    half = jax.ShapeDtypeStruct((BINS, 8, 128), jnp.float32)
    quarter = jax.ShapeDtypeStruct((HALF, 8, 128), jnp.float32)
    return pl.pallas_call(
        whiten_kernel,
        in_specs=[SMEM, pl.BlockSpec(memory_space=pltpu.VMEM), pl.BlockSpec(memory_space=pltpu.VMEM)],
        out_shape=(half, half) + (quarter,) * 4,
        compiler_params=pltpu.CompilerParams(vmem_limit_bytes=32 * 2**20),
        name="whiten",
    )(place, spectra, masks)


def stack_kernel(zh_ref, *refs):
    rows_ref, own_refs = refs[0], refs[1:5]
    cos_ref, sin_ref, out_ref, prod_ref, even_ref, odd_ref = refs[5:]
    step = pl.program_id(0)
    sign = jnp.where(lax.broadcasted_iota(jnp.int32, (4, 8, 128), 1) < 4, -1.0, 1.0)
    dot = functools.partial(jnp.dot, preferred_element_type=jnp.float32)

    def one_low(f, _):
        p = rows_ref[:, f]
        q = pltpu.roll(p, 4, axis=1) * sign
        left = jnp.concatenate([p.reshape(32, 128), q.reshape(32, 128)], axis=1)
        lh, ll = halves(left)
        left = jnp.concatenate([lh, lh, ll], axis=0).T
        for h in range(2):
            rh, rl = halves(jnp.concatenate([ref[h, f] for ref in own_refs], axis=0))
            right = jnp.concatenate([rh, rl, rh], axis=0)
            rows = jnp.concatenate([left[64 * h : 64 * h + 64], left[128 + 64 * h : 192 + 64 * h]], axis=0)
            prod_ref[2 * f + h] = dot(rows, right).reshape(2, 64, 128)
        return 0

    lax.fori_loop(0, STEP, one_low, 0, unroll=4)

    @pl.when(step == 0)
    def _():
        even_ref[...] = jnp.zeros_like(even_ref)
        odd_ref[...] = jnp.zeros_like(odd_ref)

    for t in range(4):
        for part, table_ref, sum_ref in ((0, cos_ref, even_ref), (1, sin_ref, odd_ref)):
            size = sum_ref.shape[1]
            value = jnp.concatenate(
                [prod_ref[:, part, 8 * t : 8 * t + 8], prod_ref[:, part, 32 + 8 * t : 40 + 8 * t]], axis=2
            ).reshape(STEP * 16, 256)
            vh, vl = halves(value)
            both = dot(table_ref[0], vh)
            sum_ref[t] += both[:size] + both[size:] + dot(table_ref[0, :size], vl)

    @pl.when(step == STEPS - 1)
    def _():
        mid = LAGS // 2
        for t in range(4):
            even = even_ref[t].reshape(EVEN, 8, 256)
            odd = odd_ref[t].reshape(ODD, 8, 256)
            for k in range(2):
                tile = t + 4 * k
                owner = (tile // 2) ^ zh_ref[0]
                place = pl.ds(8 * (tile % 2), 8)
                e, o = even[:, :, 128 * k : 128 * k + 128], odd[:, :, 128 * k : 128 * k + 128]
                out_ref[owner, mid, place] = e[0]
                for lag in range(1, mid + 1):
                    out_ref[owner, mid + lag, place] = e[lag] - o[lag - 1]
                    out_ref[owner, mid - lag, place] = e[lag] + o[lag - 1]


def stack(zh, rows, own, cos_t, sin_t):
    own = [piece.reshape(2, HALF, 8, 128) for piece in own]
    return pl.pallas_call(
        stack_kernel,
        grid_spec=pltpu.PrefetchScalarGridSpec(
            num_scalar_prefetch=1,
            grid=(STEPS,),
            in_specs=[pl.BlockSpec((4, STEP, 8, 128), lambda s, zh: (0, s, 0, 0))]
            + [pl.BlockSpec((2, STEP, 8, 128), lambda s, zh: (0, s, 0, 0))] * 4
            + [
                pl.BlockSpec((1,) + cos_t.shape[1:], lambda s, zh: (s, 0, 0)),
                pl.BlockSpec((1,) + sin_t.shape[1:], lambda s, zh: (s, 0, 0)),
            ],
            out_specs=pl.BlockSpec((4, LAGS + 1, 16, 128), lambda s, zh: (0, 0, 0, 0)),
            scratch_shapes=[
                pltpu.VMEM((2 * STEP, 2, 64, 128), jnp.float32),
                pltpu.VMEM((4, 8 * EVEN, 256), jnp.float32),
                pltpu.VMEM((4, 8 * ODD, 256), jnp.float32),
            ],
        ),
        out_shape=jax.ShapeDtypeStruct((4, LAGS + 1, 16, 128), jnp.float32),
        compiler_params=pltpu.CompilerParams(vmem_limit_bytes=32 * 2**20),
        cost_estimate=pl.CostEstimate(flops=8 * 10**9, bytes_accessed=8 * 2**20, transcendentals=0),
        name="stack",
    )(zh, rows, *own, cos_t, sin_t)


def pack_kernel(*refs):
    terms, sums_ref, out_ref = refs[:-2], refs[-2], refs[-1]
    per = len(terms) // 2
    block = lax.broadcasted_iota(jnp.int32, (16, 128), 1) // 16
    for r in range(2):
        own_ref, *rest = terms[per * r : per * r + per]
        total = own_ref[0]
        for ref in rest:
            total = total + ref[...]
        sums_ref[r] = total
        for g in range(4):
            found = [None] * 8
            for k in range(8):
                value = total[LAGS - 8 * g - k]
                for d in range(8):
                    turned = value if d == k else pltpu.roll(value, 16 * ((k - d) % 8), axis=1)
                    found[d] = turned if k == 0 else jnp.where(block == k, turned, found[d])
            for d in range(8):
                out_ref[d, r, g] = found[d]


def pack(terms):
    own = pl.BlockSpec((1, LAGS + 1, 16, 128), lambda s: (0, 0, 0, 0))
    specs = [own] + [pl.BlockSpec((LAGS + 1, 16, 128), lambda s: (0, 0, 0))] * 3
    return pl.pallas_call(
        pack_kernel,
        grid=(1,),
        in_specs=specs * 2,
        out_specs=(
            pl.BlockSpec((2, LAGS + 1, 16, 128), lambda s: (0, 0, 0, 0)),
            pl.BlockSpec((8, 2, 4, 16, 128), lambda s: (0, 0, 0, 0, 0)),
        ),
        out_shape=(
            jax.ShapeDtypeStruct((2, LAGS + 1, 16, 128), jnp.float32),
            jax.ShapeDtypeStruct((8, 2, 4, 16, 128), jnp.float32),
        ),
        name="pack",
    )(*terms)


def finish_kernel(flags_ref, turned_ref, first_ref, second_ref, out_ref):
    for r, straight_ref in enumerate((first_ref, second_ref)):
        near = straight_ref[0, :LAGS]
        far = jnp.concatenate(
            [turned_ref[:, r, g].reshape(128, 128).T.reshape(8, 16, 128) for g in range(4)], axis=0
        )
        left = flags_ref[0] == 0
        full = jnp.concatenate([jnp.where(left, far, near), jnp.where(left, near, far)], axis=2)
        out_ref[flags_ref[1] ^ r] = jnp.swapaxes(full, 0, 1)


def finish(flags, turned, straight):
    return pl.pallas_call(
        finish_kernel,
        in_specs=[SMEM] + [pl.BlockSpec(memory_space=pltpu.VMEM)] * 3,
        out_shape=jax.ShapeDtypeStruct((2, 16, LAGS, 256), jnp.float32),
        name="finish",
    )(flags, turned, *straight)


def chooser(low, high):
    common = low & high
    return common & -common if common else (low & -low) | (high & -high)


def by_offsets(send, low, high, *values):
    count = lax.axis_size("blk")
    branches = [functools.partial(send, a, c) for c in range(2, count) for a in range(1, c)]
    return lax.switch((high - 1) * (high - 2) // 2 + low - 1, branches, *values)


def send_rows(low, high, value):
    count = lax.axis_size("blk")
    return [lax.ppermute(value, "blk", [(b, b ^ mask) for b in range(count)]) for mask in (low, high)]


def send_sums(low, high, first, second):
    bits = chooser(low, high)
    count = lax.axis_size("blk")
    sent = []
    for mask, value in ((low, first), (high, second)):
        pairs = []
        for b in range(count):
            turn = (b & bits).bit_count() & 1
            pairs += [(2 * b + x, 2 * (b ^ mask) + (x ^ turn)) for x in range(2)]
        sent.append(lax.ppermute(value, ("blk", "xh"), pairs))
    return sent


def swap(value, axis, d):
    count = 4
    return lax.ppermute(value, axis, [(i, i ^ d) for i in range(count)])


def on_device(spectra, masks, plan):
    cos_t, sin_t = (jnp.asarray(t) for t in lag_tables())
    swapped = (plan[0, 0] > plan[1, 0]).astype(jnp.int32)
    low, high = jnp.minimum(plan[0, 0], plan[1, 0]), jnp.maximum(plan[0, 0], plan[1, 0])
    common = low & high
    bits = jnp.where(common != 0, common & -common, (low & -low) | (high & -high))
    flag = lax.population_count(bits & lax.axis_index("blk")) & 1
    side = lax.axis_index("xh")
    zh = lax.axis_index("zh")[None]
    x = ("xh", "xl")
    place = jnp.stack([side, (2 * side + lax.axis_index("xl")) ^ (2 - 2 * flag)])
    near, far, *rows = whiten(place, spectra, masks)
    rows = [rows[0]] + [swap(rows[d], x, d) for d in (1, 2, 3)]
    own = [near] + [swap(near if d == 1 else far, x, d) for d in (1, 2, 3)]
    theirs = by_offsets(send_rows, low, high, jnp.stack(rows, axis=0))
    terms = []
    for r in range(2):
        partial = stack(zh, theirs[r], own, cos_t, sin_t)
        terms += [partial] + [swap(partial[d], "zh", d) for d in (1, 2, 3)]
    sums, turned = pack(terms)
    turned = lax.all_to_all(turned, ("xl", "zh"), split_axis=0, concat_axis=0, tiled=True)
    straight = by_offsets(send_sums, low, high, sums[:1], sums[1:])
    return finish(jnp.stack([side ^ flag, swapped]), turned, straight)


def solution(mesh):
    fine = Mesh(mesh.devices.reshape(16, 2, 2, 4), ("blk", "xh", "xl", "zh"))
    return jax.shard_map(
        on_device,
        mesh=fine,
        in_specs=(P(None, ("xh", "xl", "zh"), None, "blk"), P(("xh", "xl", "zh"), "blk"), P()),
        out_specs=P(None, ("blk", "xh", "xl", "zh"), None, None),
        check_vma=False,
    )
```

```python
import functools
import math

import jax
import jax.numpy as jnp
import ml_dtypes
import numpy as np
from jax import lax
from jax.experimental import pallas as pl
from jax.experimental.pallas import tpu as pltpu
from jax.sharding import Mesh
from jax.sharding import PartitionSpec as P

LAGS = 32
BINS = 192
WINDOWS = 64
HALF = BINS // 2
STEP = 16
STEPS = HALF // STEP
EVEN = 18
ODD = 16
SMEM = pl.BlockSpec(memory_space=pltpu.SMEM)


def lag_tables():
    norm = 1.0 / math.sqrt(WINDOWS * BINS)
    bins = np.arange(BINS).reshape(2, STEPS, STEP).transpose(1, 2, 0)
    tables = []
    for turn, lags in ((np.cos, np.arange(EVEN)), (np.sin, np.arange(1, ODD + 1))):
        wave = turn(np.pi * bins[..., None] * lags / BINS) * norm * (lags <= LAGS // 2)
        table = np.einsum("sfhl,jk->sljfhk", wave, np.eye(8))
        table = table.reshape(STEPS, 8 * len(lags), STEP * 2 * 8).astype(np.float32)
        high = table.astype(ml_dtypes.bfloat16)
        low = (table - high.astype(np.float32)).astype(ml_dtypes.bfloat16)
        tables.append(np.concatenate([high, low], axis=1))
    return tables


def halves(value):
    high = value.astype(jnp.bfloat16)
    return high, (value - high.astype(jnp.float32)).astype(jnp.bfloat16)


def whiten_kernel(place_ref, spectra_ref, masks_ref, near_ref, far_ref, *rows_refs):
    parts, windows, bins, channels = spectra_ref.shape
    pieces = []
    scales = []
    for w in range(windows):
        a, b = spectra_ref[0, w], spectra_ref[1, w]
        power = jnp.sum(a * a + b * b, axis=0, keepdims=True) * (1.0 / bins)
        scales.append(masks_ref[w : w + 1, :].astype(jnp.float32) * lax.rsqrt(power + 1e-06))
    for p in range(parts):
        for w in range(windows):
            pieces.append(spectra_ref[p, w] * scales[w])
    white = jnp.swapaxes(jnp.stack(pieces, axis=0), 0, 1)
    lane = lax.broadcasted_iota(jnp.int32, (HALF, 8, 128), 2)

    for side in range(2):

        @pl.when(place_ref[0] == side)
        def _():
            near_ref[...] = white[:, :, side * 128 : side * 128 + 128]
            far_ref[...] = white[:, :, 128 - side * 128 : 256 - side * 128]

    quarters = []
    for block in range(channels // 128):
        a = white[:HALF, :, block * 128 : (block + 1) * 128]
        b = white[HALF:, :, block * 128 : (block + 1) * 128]
        quarters.append(jnp.where(lane < 64, a, pltpu.roll(b, 64, axis=2)))
        quarters.append(jnp.where(lane < 64, pltpu.roll(a, 64, axis=2), b))
    for own in range(4):

        @pl.when(place_ref[1] == own)
        def _():
            for quarter in range(4):
                rows_refs[quarter ^ own][...] = quarters[quarter]


def whiten(place, spectra, masks):
    half = jax.ShapeDtypeStruct((BINS, 8, 128), jnp.float32)
    quarter = jax.ShapeDtypeStruct((HALF, 8, 128), jnp.float32)
    return pl.pallas_call(
        whiten_kernel,
        in_specs=[SMEM, pl.BlockSpec(memory_space=pltpu.VMEM), pl.BlockSpec(memory_space=pltpu.VMEM)],
        out_shape=(half, half) + (quarter,) * 4,
        compiler_params=pltpu.CompilerParams(vmem_limit_bytes=32 * 2**20),
        name="whiten",
    )(place, spectra, masks)


def stack_kernel(zh_ref, *refs):
    rows_ref, own_refs = refs[0], refs[1:5]
    cos_ref, sin_ref, out_ref, prod_ref, even_ref, odd_ref = refs[5:]
    step = pl.program_id(0)
    sign = jnp.where(lax.broadcasted_iota(jnp.int32, (4, 8, 128), 1) < 4, -1.0, 1.0)
    dot = functools.partial(jnp.dot, preferred_element_type=jnp.float32)

    def one_low(f, _):
        p = rows_ref[:, f]
        q = pltpu.roll(p, 4, axis=1) * sign
        left = jnp.concatenate([p.reshape(32, 128), q.reshape(32, 128)], axis=1)
        lh, ll = halves(left)
        left = jnp.concatenate([lh, lh, ll], axis=0).T
        for h in range(2):
            rh, rl = halves(jnp.concatenate([ref[h, f] for ref in own_refs], axis=0))
            right = jnp.concatenate([rh, rl, rh], axis=0)
            rows = jnp.concatenate([left[64 * h : 64 * h + 64], left[128 + 64 * h : 192 + 64 * h]], axis=0)
            prod_ref[2 * f + h] = dot(rows, right).reshape(2, 64, 128)
        return 0

    lax.fori_loop(0, STEP, one_low, 0, unroll=4)

    @pl.when(step == 0)
    def _():
        even_ref[...] = jnp.zeros_like(even_ref)
        odd_ref[...] = jnp.zeros_like(odd_ref)

    for t in range(4):
        for part, table_ref, sum_ref in ((0, cos_ref, even_ref), (1, sin_ref, odd_ref)):
            size = sum_ref.shape[1]
            value = jnp.concatenate(
                [prod_ref[:, part, 8 * t : 8 * t + 8], prod_ref[:, part, 32 + 8 * t : 40 + 8 * t]], axis=2
            ).reshape(STEP * 16, 256)
            vh, vl = halves(value)
            both = dot(table_ref[0], vh)
            sum_ref[t] += both[:size] + both[size:] + dot(table_ref[0, :size], vl)

    @pl.when(step == STEPS - 1)
    def _():
        mid = LAGS // 2
        for t in range(4):
            even = even_ref[t].reshape(EVEN, 8, 256)
            odd = odd_ref[t].reshape(ODD, 8, 256)
            for k in range(2):
                tile = t + 4 * k
                owner = (tile // 2) ^ zh_ref[0]
                place = pl.ds(8 * (tile % 2), 8)
                e, o = even[:, :, 128 * k : 128 * k + 128], odd[:, :, 128 * k : 128 * k + 128]
                out_ref[owner, mid, place] = e[0]
                for lag in range(1, mid + 1):
                    out_ref[owner, mid + lag, place] = e[lag] - o[lag - 1]
                    out_ref[owner, mid - lag, place] = e[lag] + o[lag - 1]


def stack(zh, rows, own, cos_t, sin_t):
    own = [piece.reshape(2, HALF, 8, 128) for piece in own]
    return pl.pallas_call(
        stack_kernel,
        grid_spec=pltpu.PrefetchScalarGridSpec(
            num_scalar_prefetch=1,
            grid=(STEPS,),
            in_specs=[pl.BlockSpec((4, STEP, 8, 128), lambda s, zh: (0, s, 0, 0))]
            + [pl.BlockSpec((2, STEP, 8, 128), lambda s, zh: (0, s, 0, 0))] * 4
            + [
                pl.BlockSpec((1,) + cos_t.shape[1:], lambda s, zh: (s, 0, 0)),
                pl.BlockSpec((1,) + sin_t.shape[1:], lambda s, zh: (s, 0, 0)),
            ],
            out_specs=pl.BlockSpec((4, LAGS + 1, 16, 128), lambda s, zh: (0, 0, 0, 0)),
            scratch_shapes=[
                pltpu.VMEM((2 * STEP, 2, 64, 128), jnp.float32),
                pltpu.VMEM((4, 8 * EVEN, 256), jnp.float32),
                pltpu.VMEM((4, 8 * ODD, 256), jnp.float32),
            ],
        ),
        out_shape=jax.ShapeDtypeStruct((4, LAGS + 1, 16, 128), jnp.float32),
        compiler_params=pltpu.CompilerParams(vmem_limit_bytes=32 * 2**20),
        cost_estimate=pl.CostEstimate(flops=8 * 10**9, bytes_accessed=8 * 2**20, transcendentals=0),
        name="stack",
    )(zh, rows, *own, cos_t, sin_t)


def pack_kernel(side_ref, own_ref, *refs):
    terms, sums_ref, out_ref = refs[:-2], refs[-2], refs[-1]
    block = lax.broadcasted_iota(jnp.int32, (16, 128), 1) // 16
    total = own_ref[0]
    for ref in terms:
        total = total + ref[...]
    sums_ref[...] = total
    out_ref[1 - side_ref[0]] = jnp.zeros(out_ref.shape[1:], jnp.float32)
    for g in range(4):
        found = [None] * 8
        for k in range(8):
            value = total[LAGS - 8 * g - k]
            for d in range(8):
                turned = value if d == k else pltpu.roll(value, 16 * ((k - d) % 8), axis=1)
                found[d] = turned if k == 0 else jnp.where(block == k, turned, found[d])
        for d in range(8):
            out_ref[side_ref[0], d, g] = found[d]


def pack(side, terms):
    piece = pl.BlockSpec((LAGS + 1, 16, 128), lambda s, side: (0, 0, 0))
    return pl.pallas_call(
        pack_kernel,
        grid_spec=pltpu.PrefetchScalarGridSpec(
            num_scalar_prefetch=1,
            grid=(1,),
            in_specs=[pl.BlockSpec((1, LAGS + 1, 16, 128), lambda s, side: (0, 0, 0, 0))] + [piece] * 3,
            out_specs=(piece, pl.BlockSpec((2, 8, 4, 16, 128), lambda s, side: (0, 0, 0, 0, 0))),
        ),
        out_shape=(
            jax.ShapeDtypeStruct((LAGS + 1, 16, 128), jnp.float32),
            jax.ShapeDtypeStruct((2, 8, 4, 16, 128), jnp.float32),
        ),
        cost_estimate=pl.CostEstimate(flops=10**6, bytes_accessed=2 * 2**20, transcendentals=0),
        name="pack",
    )(side, *terms)


def finish_kernel(side_ref, *refs):
    out_ref = refs[-1]
    for r in range(2):
        straight_ref, turned_ref = refs[2 * r : 2 * r + 2]
        near = straight_ref[:LAGS]
        turned = turned_ref[side_ref[0]]
        far = jnp.concatenate([turned[:, g].reshape(128, 128).T.reshape(8, 16, 128) for g in range(4)], axis=0)
        left = side_ref[0] == 0
        full = jnp.concatenate([jnp.where(left, far, near), jnp.where(left, near, far)], axis=2)
        out_ref[r] = jnp.swapaxes(full, 0, 1)


def finish(side, pieces):
    return pl.pallas_call(
        finish_kernel,
        in_specs=[SMEM] + [pl.BlockSpec(memory_space=pltpu.VMEM)] * 4,
        out_shape=jax.ShapeDtypeStruct((2, 16, LAGS, 256), jnp.float32),
        name="finish",
    )(side, *pieces)


def to_partner(mask, value):
    return lax.ppermute(value, "blk", [(b, b ^ mask) for b in range(lax.axis_size("blk"))])


def by_offset(branch, offset, *values):
    count = lax.axis_size("blk")
    return lax.switch(offset - 1, [functools.partial(branch, mask) for mask in range(1, count)], *values)


def swap(value, axis, d):
    return lax.ppermute(value, axis, [(i, i ^ d) for i in range(4)])


def on_device(spectra, masks, plan):
    tables = [jnp.asarray(t) for t in lag_tables()]
    common = plan[0, 0] & plan[1, 0]
    bits = jnp.where(common != 0, common & -common, (plan[0, 0] & -plan[0, 0]) | (plan[1, 0] & -plan[1, 0]))
    flag = lax.population_count(bits & lax.axis_index("blk")) & 1
    side = lax.axis_index("xh") ^ flag
    zh = lax.axis_index("zh")[None]
    x = ("xh", "xl")
    near, far, *rows = whiten(jnp.stack([side, lax.axis_index(x)]), spectra, masks)
    rows = jnp.stack([rows[0]] + [swap(rows[d], x, d) for d in (1, 2, 3)], axis=0)
    near, far, rows = lax.optimization_barrier((near, far, rows))
    own = [near] + [swap(near if d == 1 else far, x, d) for d in (1, 2, 3)]

    def fetch(mask, rows):
        return to_partner(mask, rows)

    def fetch_and_stack(mask, rows, theirs, zh, own, tables):
        return to_partner(mask, rows), stack(zh, theirs, own, *tables)

    first = by_offset(fetch, plan[0, 0], rows)
    second, partial = by_offset(fetch_and_stack, plan[1, 0], rows, first, zh, own, tables)
    terms = [[partial] + [swap(partial[d], "zh", d) for d in (1, 2, 3)]]
    partial = stack(zh, second, own, *tables)
    terms.append([partial] + [swap(partial[d], "zh", d) for d in (1, 2, 3)])
    pieces = []
    for r in range(2):
        sums, turned = pack(side[None], terms[r])
        turned = lax.all_to_all(
            turned.reshape(16, 4, 16, 128), ("xh", "xl", "zh"), split_axis=0, concat_axis=0, tiled=True
        )
        pieces += [by_offset(to_partner, plan[r, 0], sums), turned.reshape(2, 8, 4, 16, 128)]
    return finish(side[None], pieces)


def solution(mesh):
    fine = Mesh(mesh.devices.reshape(16, 2, 2, 4), ("blk", "xh", "xl", "zh"))
    return jax.shard_map(
        on_device,
        mesh=fine,
        in_specs=(P(None, ("xh", "xl", "zh"), None, "blk"), P(("xh", "xl", "zh"), "blk"), P()),
        out_specs=P(None, ("blk", "xh", "xl", "zh"), None, None),
        check_vma=False,
    )
```

```python
import functools
import math

import jax
import jax.numpy as jnp
import ml_dtypes
import numpy as np
from jax import lax
from jax.experimental import pallas as pl
from jax.experimental.pallas import tpu as pltpu
from jax.sharding import Mesh
from jax.sharding import PartitionSpec as P

LAGS = 32
BINS = 192
WINDOWS = 64
HALF = BINS // 2
STEP = 16
STEPS = HALF // STEP
EVEN = 18
ODD = 16
SMEM = pl.BlockSpec(memory_space=pltpu.SMEM)


def lag_tables():
    norm = 1.0 / math.sqrt(WINDOWS * BINS)
    bins = np.arange(BINS).reshape(2, STEPS, STEP).transpose(1, 2, 0)
    tables = []
    for turn, lags in ((np.cos, np.arange(EVEN)), (np.sin, np.arange(1, ODD + 1))):
        wave = turn(np.pi * bins[..., None] * lags / BINS) * norm * (lags <= LAGS // 2)
        table = np.einsum("sfhl,jk->sljfhk", wave, np.eye(8))
        table = table.reshape(STEPS, 8 * len(lags), STEP * 2 * 8).astype(np.float32)
        high = table.astype(ml_dtypes.bfloat16)
        low = (table - high.astype(np.float32)).astype(ml_dtypes.bfloat16)
        tables.append(np.concatenate([high, low], axis=1))
    return tables


def halves(value):
    high = value.astype(jnp.bfloat16)
    return high, (value - high.astype(jnp.float32)).astype(jnp.bfloat16)


def chooser(first, second):
    common = first & second
    return jnp.where(common != 0, common & -common, (first & -first) | (second & -second))


def parity(bits):
    bits = bits ^ (bits >> 2)
    return (bits ^ (bits >> 1)) & 1


def whiten_kernel(spectra_ref, masks_ref, own_ref, rows_ref):
    parts, windows, bins, channels = spectra_ref.shape
    x = 2 * lax.axis_index("xh") + lax.axis_index("xl")
    pieces = []
    scales = []
    for w in range(windows):
        a, b = spectra_ref[0, w], spectra_ref[1, w]
        power = jnp.sum(a * a + b * b, axis=0, keepdims=True) * (1.0 / bins)
        scales.append(masks_ref[w : w + 1, :].astype(jnp.float32) * lax.rsqrt(power + 1e-06))
    for p in range(parts):
        for w in range(windows):
            pieces.append(spectra_ref[p, w] * scales[w])
    white = jnp.swapaxes(jnp.stack(pieces, axis=0), 0, 1)
    own_ref[...] = white
    lane = lax.broadcasted_iota(jnp.int32, (HALF, 8, 128), 2)
    for block in range(channels // 128):
        a = white[:HALF, :, block * 128 : (block + 1) * 128]
        b = white[HALF:, :, block * 128 : (block + 1) * 128]
        rows_ref[(2 * block) ^ x] = jnp.where(lane < 64, a, pltpu.roll(b, 64, axis=2))
        rows_ref[(2 * block + 1) ^ x] = jnp.where(lane < 64, pltpu.roll(a, 64, axis=2), b)


def whiten(spectra, masks):
    return pl.pallas_call(
        whiten_kernel,
        out_shape=(
            jax.ShapeDtypeStruct((BINS, 8, 256), jnp.float32),
            jax.ShapeDtypeStruct((4, HALF, 8, 128), jnp.float32),
        ),
        compiler_params=pltpu.CompilerParams(vmem_limit_bytes=32 * 2**20),
        name="whiten",
    )(spectra, masks)


def stack_kernel(place_ref, own_rows_ref, *refs):
    rows_refs, own_refs = refs[:3], refs[3:7]
    cos_ref, sin_ref, out_ref, prod_ref, even_ref, odd_ref = refs[7:]
    step = pl.program_id(0)
    sign = jnp.where(lax.broadcasted_iota(jnp.int32, (4, 8, 128), 1) < 4, -1.0, 1.0)
    dot = functools.partial(jnp.dot, preferred_element_type=jnp.float32)

    def one_low(f, _):
        p = jnp.stack([own_rows_ref[0, f]] + [ref[f] for ref in rows_refs], axis=0)
        q = pltpu.roll(p, 4, axis=1) * sign
        left = jnp.concatenate([p.reshape(32, 128), q.reshape(32, 128)], axis=1)
        lh, ll = halves(left)
        left = jnp.concatenate([lh, lh, ll], axis=0).T
        for h in range(2):
            rh, rl = halves(jnp.concatenate([ref[0, h, f] for ref in own_refs], axis=0))
            right = jnp.concatenate([rh, rl, rh], axis=0)
            rows = jnp.concatenate([left[64 * h : 64 * h + 64], left[128 + 64 * h : 192 + 64 * h]], axis=0)
            prod_ref[2 * f + h] = dot(rows, right).reshape(2, 64, 128)
        return 0

    lax.fori_loop(0, STEP, one_low, 0, unroll=4)

    @pl.when(step == 0)
    def _():
        even_ref[...] = jnp.zeros_like(even_ref)
        odd_ref[...] = jnp.zeros_like(odd_ref)

    for t in range(4):
        for part, table_ref, sum_ref in ((0, cos_ref, even_ref), (1, sin_ref, odd_ref)):
            size = sum_ref.shape[1]
            value = jnp.concatenate(
                [prod_ref[:, part, 8 * t : 8 * t + 8], prod_ref[:, part, 32 + 8 * t : 40 + 8 * t]], axis=2
            ).reshape(STEP * 16, 256)
            vh, vl = halves(value)
            both = dot(table_ref[0], vh)
            sum_ref[t] += both[:size] + both[size:] + dot(table_ref[0, :size], vl)

    @pl.when(step == STEPS - 1)
    def _():
        mid = LAGS // 2
        for t in range(4):
            even = even_ref[t].reshape(EVEN, 8, 256)
            odd = odd_ref[t].reshape(ODD, 8, 256)
            for k in range(2):
                tile = t + 4 * k
                owner = (tile // 2) ^ place_ref[0]
                place = pl.ds(8 * (tile % 2), 8)
                e, o = even[:, :, 128 * k : 128 * k + 128], odd[:, :, 128 * k : 128 * k + 128]
                out_ref[owner, mid, place] = e[0]
                for lag in range(1, mid + 1):
                    out_ref[owner, mid + lag, place] = e[lag] - o[lag - 1]
                    out_ref[owner, mid - lag, place] = e[lag] + o[lag - 1]


def stack(place, rows, own, cos_t, sin_t):
    own = own.reshape(4, 2, HALF, 8, 256)

    def window(d):
        return pl.BlockSpec((1, 2, STEP, 8, 128), lambda s, place: (place[1] ^ d, 0, s, 0, place[2]))

    return pl.pallas_call(
        stack_kernel,
        grid_spec=pltpu.PrefetchScalarGridSpec(
            num_scalar_prefetch=1,
            grid=(STEPS,),
            in_specs=[pl.BlockSpec((1, STEP, 8, 128), lambda s, place: (0, s, 0, 0))]
            + [pl.BlockSpec((STEP, 8, 128), lambda s, place: (s, 0, 0))] * 3
            + [window(d) for d in range(4)]
            + [
                pl.BlockSpec((1,) + cos_t.shape[1:], lambda s, place: (s, 0, 0)),
                pl.BlockSpec((1,) + sin_t.shape[1:], lambda s, place: (s, 0, 0)),
            ],
            out_specs=pl.BlockSpec((4, LAGS + 1, 16, 128), lambda s, place: (0, 0, 0, 0)),
            scratch_shapes=[
                pltpu.VMEM((2 * STEP, 2, 64, 128), jnp.float32),
                pltpu.VMEM((4, 8 * EVEN, 256), jnp.float32),
                pltpu.VMEM((4, 8 * ODD, 256), jnp.float32),
            ],
        ),
        out_shape=jax.ShapeDtypeStruct((4, LAGS + 1, 16, 128), jnp.float32),
        compiler_params=pltpu.CompilerParams(vmem_limit_bytes=32 * 2**20),
        cost_estimate=pl.CostEstimate(flops=8 * 10**9, bytes_accessed=8 * 2**20, transcendentals=0),
        name="stack",
    )(place, *rows, *[own] * 4, cos_t, sin_t)


def pack_kernel(side_ref, own_ref, *refs):
    terms, sums_ref, out_ref = refs[:-2], refs[-2], refs[-1]
    block = lax.broadcasted_iota(jnp.int32, (16, 128), 1) // 16
    total = own_ref[0]
    for ref in terms:
        total = total + ref[...]
    sums_ref[...] = total
    out_ref[1 - side_ref[0]] = jnp.zeros(out_ref.shape[1:], jnp.float32)
    for g in range(4):
        found = [None] * 8
        for k in range(8):
            value = total[LAGS - 8 * g - k]
            for d in range(8):
                turned = value if d == k else pltpu.roll(value, 16 * ((k - d) % 8), axis=1)
                found[d] = turned if k == 0 else jnp.where(block == k, turned, found[d])
        for d in range(8):
            out_ref[side_ref[0], d, g] = found[d]


def pack(side, terms):
    piece = pl.BlockSpec((LAGS + 1, 16, 128), lambda s, side: (0, 0, 0))
    return pl.pallas_call(
        pack_kernel,
        grid_spec=pltpu.PrefetchScalarGridSpec(
            num_scalar_prefetch=1,
            grid=(1,),
            in_specs=[pl.BlockSpec((1, LAGS + 1, 16, 128), lambda s, side: (0, 0, 0, 0))] + [piece] * 3,
            out_specs=(piece, pl.BlockSpec((2, 8, 4, 16, 128), lambda s, side: (0, 0, 0, 0, 0))),
        ),
        out_shape=(
            jax.ShapeDtypeStruct((LAGS + 1, 16, 128), jnp.float32),
            jax.ShapeDtypeStruct((2, 8, 4, 16, 128), jnp.float32),
        ),
        cost_estimate=pl.CostEstimate(flops=10**6, bytes_accessed=2 * 2**20, transcendentals=0),
        name="pack",
    )(side, *terms)


def finish_kernel(side_ref, *refs):
    out_ref = refs[-1]
    for r in range(2):
        straight_ref, turned_ref = refs[2 * r : 2 * r + 2]
        near = straight_ref[:LAGS]
        turned = turned_ref[side_ref[0]]
        far = jnp.concatenate([turned[:, g].reshape(128, 128).T.reshape(8, 16, 128) for g in range(4)], axis=0)
        left = side_ref[0] == 0
        full = jnp.concatenate([jnp.where(left, far, near), jnp.where(left, near, far)], axis=2)
        out_ref[r] = jnp.swapaxes(full, 0, 1)


def finish(side, pieces):
    return pl.pallas_call(
        finish_kernel,
        in_specs=[SMEM] + [pl.BlockSpec(memory_space=pltpu.VMEM)] * 4,
        out_shape=jax.ShapeDtypeStruct((2, 16, LAGS, 256), jnp.float32),
        name="finish",
    )(side, *pieces)


def to_partner(mask, value):
    return lax.ppermute(value, "blk", [(b, b ^ mask) for b in range(lax.axis_size("blk"))])


def by_offset(branch, offset, *values):
    count = lax.axis_size("blk")
    return lax.switch(offset - 1, [functools.partial(branch, mask) for mask in range(1, count)], *values)


def swap(value, axis, d):
    return lax.ppermute(value, axis, [(i, i ^ d) for i in range(4)])


def on_device(spectra, masks, plan):
    tables = [jnp.asarray(t) for t in lag_tables()]
    own, rows = whiten(spectra, masks)
    x = ("xh", "xl")
    own = lax.all_gather(own, x, axis=0, tiled=False)
    side = lax.axis_index("xh") ^ parity(chooser(plan[0, 0], plan[1, 0]) & lax.axis_index("blk"))
    place = jnp.stack([lax.axis_index("zh"), lax.axis_index(x), side])
    order = lax.optimization_barrier
    theirs = by_offset(to_partner, plan[0, 0], rows)
    first = [theirs] + [swap(theirs[d], x, d) for d in (1, 2, 3)]
    theirs, rows = order((theirs, rows))
    theirs = by_offset(to_partner, plan[1, 0], rows)
    second = [theirs] + [swap(theirs[d], x, d) for d in (1, 2, 3)]

    def exchanged(partial):
        return [partial] + [swap(partial[d], "zh", d) for d in (1, 2, 3)]

    def sent(terms, r):
        sums, turned = pack(side[None], terms)
        turned = turned.reshape(16, 4, 16, 128)
        turned = lax.all_to_all(turned, ("xh", "xl", "zh"), split_axis=0, concat_axis=0, tiled=True)
        return [by_offset(to_partner, plan[r, 0], sums), turned.reshape(2, 8, 4, 16, 128)]

    first, theirs = order((first, theirs))
    early = exchanged(stack(place, first, own, *tables))
    late = stack(place, second, own, *tables)
    early, late = order((early, late))
    late = exchanged(late)
    early = sent(early, 0)
    early, late = order((early, late))
    return finish(side[None], early + sent(late, 1))


def solution(mesh):
    fine = Mesh(mesh.devices.reshape(16, 2, 2, 4), ("blk", "xh", "xl", "zh"))
    return jax.shard_map(
        on_device,
        mesh=fine,
        in_specs=(P(None, ("xh", "xl", "zh"), None, "blk"), P(("xh", "xl", "zh"), "blk"), P()),
        out_specs=P(None, ("blk", "xh", "xl", "zh"), None, None),
        check_vma=False,
    )
```

```python
import functools
import math

import jax
import jax.numpy as jnp
import ml_dtypes
import numpy as np
from jax import lax
from jax.experimental import pallas as pl
from jax.experimental.pallas import tpu as pltpu
from jax.sharding import Mesh
from jax.sharding import PartitionSpec as P

LAGS = 32
BINS = 192
WINDOWS = 64
HALF = BINS // 2
STEP = 16
STEPS = HALF // STEP
EVEN = 18
ODD = 16
SMEM = pl.BlockSpec(memory_space=pltpu.SMEM)


def lag_tables():
    norm = 1.0 / math.sqrt(WINDOWS * BINS)
    bins = np.arange(BINS).reshape(2, STEPS, STEP).transpose(1, 2, 0)
    tables = []
    for turn, lags in ((np.cos, np.arange(EVEN)), (np.sin, np.arange(1, ODD + 1))):
        wave = turn(np.pi * bins[..., None] * lags / BINS) * norm * (lags <= LAGS // 2)
        table = np.einsum("sfhl,jk->sljfhk", wave, np.eye(8))
        table = table.reshape(STEPS, 8 * len(lags), STEP * 2 * 8).astype(np.float32)
        high = table.astype(ml_dtypes.bfloat16)
        low = (table - high.astype(np.float32)).astype(ml_dtypes.bfloat16)
        tables.append(np.concatenate([high, low], axis=1))
    return tables


def halves(value):
    high = value.astype(jnp.bfloat16)
    return high, (value - high.astype(jnp.float32)).astype(jnp.bfloat16)


def chooser(first, second):
    common = first & second
    return jnp.where(common != 0, common & -common, (first & -first) | (second & -second))


def parity(bits):
    bits = bits ^ (bits >> 2)
    return (bits ^ (bits >> 1)) & 1


def whiten_kernel(spectra_ref, masks_ref, own_ref, rows_ref):
    parts, windows, bins, channels = spectra_ref.shape
    x = 2 * lax.axis_index("xh") + lax.axis_index("xl")
    pieces = []
    scales = []
    for w in range(windows):
        a, b = spectra_ref[0, w], spectra_ref[1, w]
        power = jnp.sum(a * a + b * b, axis=0, keepdims=True) * (1.0 / bins)
        scales.append(masks_ref[w : w + 1, :].astype(jnp.float32) * lax.rsqrt(power + 1e-06))
    for p in range(parts):
        for w in range(windows):
            pieces.append(spectra_ref[p, w] * scales[w])
    white = jnp.swapaxes(jnp.stack(pieces, axis=0), 0, 1)
    own_ref[...] = white
    lane = lax.broadcasted_iota(jnp.int32, (HALF, 8, 128), 2)
    for block in range(channels // 128):
        a = white[:HALF, :, block * 128 : (block + 1) * 128]
        b = white[HALF:, :, block * 128 : (block + 1) * 128]
        rows_ref[(2 * block) ^ x] = jnp.where(lane < 64, a, pltpu.roll(b, 64, axis=2))
        rows_ref[(2 * block + 1) ^ x] = jnp.where(lane < 64, pltpu.roll(a, 64, axis=2), b)


def whiten(spectra, masks):
    return pl.pallas_call(
        whiten_kernel,
        out_shape=(
            jax.ShapeDtypeStruct((BINS, 8, 256), jnp.float32),
            jax.ShapeDtypeStruct((4, HALF, 8, 128), jnp.float32),
        ),
        compiler_params=pltpu.CompilerParams(vmem_limit_bytes=32 * 2**20),
        name="whiten",
    )(spectra, masks)


def stack_kernel(place_ref, own_rows_ref, *refs):
    rows_refs, own_refs = refs[:3], refs[3:7]
    cos_ref, sin_ref, out_ref, prod_ref, even_ref, odd_ref = refs[7:]
    step = pl.program_id(0)
    sign = jnp.where(lax.broadcasted_iota(jnp.int32, (4, 8, 128), 1) < 4, -1.0, 1.0)
    dot = functools.partial(jnp.dot, preferred_element_type=jnp.float32)

    def one_low(f, _):
        p = jnp.stack([own_rows_ref[0, f]] + [ref[f] for ref in rows_refs], axis=0)
        q = pltpu.roll(p, 4, axis=1) * sign
        left = jnp.concatenate([p.reshape(32, 128), q.reshape(32, 128)], axis=1)
        lh, ll = halves(left)
        left = jnp.concatenate([lh, lh, ll], axis=0).T
        for h in range(2):
            rh, rl = halves(jnp.concatenate([ref[0, h, f] for ref in own_refs], axis=0))
            right = jnp.concatenate([rh, rl, rh], axis=0)
            rows = jnp.concatenate([left[64 * h : 64 * h + 64], left[128 + 64 * h : 192 + 64 * h]], axis=0)
            prod_ref[2 * f + h] = dot(rows, right).reshape(2, 64, 128)
        return 0

    lax.fori_loop(0, STEP, one_low, 0, unroll=4)

    @pl.when(step == 0)
    def _():
        even_ref[...] = jnp.zeros_like(even_ref)
        odd_ref[...] = jnp.zeros_like(odd_ref)

    for t in range(4):
        for part, table_ref, sum_ref in ((0, cos_ref, even_ref), (1, sin_ref, odd_ref)):
            size = sum_ref.shape[1]
            value = jnp.concatenate(
                [prod_ref[:, part, 8 * t : 8 * t + 8], prod_ref[:, part, 32 + 8 * t : 40 + 8 * t]], axis=2
            ).reshape(STEP * 16, 256)
            vh, vl = halves(value)
            both = dot(table_ref[0], vh)
            sum_ref[t] += both[:size] + both[size:] + dot(table_ref[0, :size], vl)

    @pl.when(step == STEPS - 1)
    def _():
        mid = LAGS // 2
        for t in range(4):
            even = even_ref[t].reshape(EVEN, 8, 256)
            odd = odd_ref[t].reshape(ODD, 8, 256)
            for k in range(2):
                tile = t + 4 * k
                owner = (tile // 2) ^ place_ref[0]
                place = pl.ds(8 * (tile % 2), 8)
                e, o = even[:, :, 128 * k : 128 * k + 128], odd[:, :, 128 * k : 128 * k + 128]
                out_ref[owner, mid, place] = e[0]
                for lag in range(1, mid + 1):
                    out_ref[owner, mid + lag, place] = e[lag] - o[lag - 1]
                    out_ref[owner, mid - lag, place] = e[lag] + o[lag - 1]


def stack(place, rows, own, cos_t, sin_t):
    own = own.reshape(4, 2, HALF, 8, 256)

    def window(d):
        return pl.BlockSpec((1, 2, STEP, 8, 128), lambda s, place: (place[1] ^ d, 0, s, 0, place[2]))

    return pl.pallas_call(
        stack_kernel,
        grid_spec=pltpu.PrefetchScalarGridSpec(
            num_scalar_prefetch=1,
            grid=(STEPS,),
            in_specs=[pl.BlockSpec((1, STEP, 8, 128), lambda s, place: (0, s, 0, 0))]
            + [pl.BlockSpec((STEP, 8, 128), lambda s, place: (s, 0, 0))] * 3
            + [window(d) for d in range(4)]
            + [
                pl.BlockSpec((1,) + cos_t.shape[1:], lambda s, place: (s, 0, 0)),
                pl.BlockSpec((1,) + sin_t.shape[1:], lambda s, place: (s, 0, 0)),
            ],
            out_specs=pl.BlockSpec((4, LAGS + 1, 16, 128), lambda s, place: (0, 0, 0, 0)),
            scratch_shapes=[
                pltpu.VMEM((2 * STEP, 2, 64, 128), jnp.float32),
                pltpu.VMEM((4, 8 * EVEN, 256), jnp.float32),
                pltpu.VMEM((4, 8 * ODD, 256), jnp.float32),
            ],
        ),
        out_shape=jax.ShapeDtypeStruct((4, LAGS + 1, 16, 128), jnp.float32),
        compiler_params=pltpu.CompilerParams(vmem_limit_bytes=32 * 2**20),
        cost_estimate=pl.CostEstimate(flops=8 * 10**9, bytes_accessed=8 * 2**20, transcendentals=0),
        name="stack",
    )(place, *rows, *[own] * 4, cos_t, sin_t)


def pack_kernel(side_ref, first_ref, own_ref, *refs):
    terms, sums_ref, out_ref = refs[:-2], refs[-2], refs[-1]
    block = lax.broadcasted_iota(jnp.int32, (16, 128), 1) // 16
    total = own_ref[0]
    for ref in terms:
        total = total + ref[...]
    sums_ref[...] = total
    out_ref[1 - side_ref[0]] = jnp.zeros(out_ref.shape[1:], jnp.float32)
    for r, sums in enumerate((first_ref[...], total)):
        for g in range(4):
            found = [None] * 8
            for k in range(8):
                value = sums[LAGS - 8 * g - k]
                for d in range(8):
                    turned = value if d == k else pltpu.roll(value, 16 * ((k - d) % 8), axis=1)
                    found[d] = turned if k == 0 else jnp.where(block == k, turned, found[d])
            for d in range(8):
                out_ref[side_ref[0], d, r, g] = found[d]


def pack(side, first, terms):
    piece = pl.BlockSpec((LAGS + 1, 16, 128), lambda s, side: (0, 0, 0))
    return pl.pallas_call(
        pack_kernel,
        grid_spec=pltpu.PrefetchScalarGridSpec(
            num_scalar_prefetch=1,
            grid=(1,),
            in_specs=[piece, pl.BlockSpec((1, LAGS + 1, 16, 128), lambda s, side: (0, 0, 0, 0))] + [piece] * 3,
            out_specs=(piece, pl.BlockSpec((2, 8, 2, 4, 16, 128), lambda s, side: (0, 0, 0, 0, 0, 0))),
        ),
        out_shape=(
            jax.ShapeDtypeStruct((LAGS + 1, 16, 128), jnp.float32),
            jax.ShapeDtypeStruct((2, 8, 2, 4, 16, 128), jnp.float32),
        ),
        cost_estimate=pl.CostEstimate(flops=10**6, bytes_accessed=3 * 2**20, transcendentals=0),
        name="pack",
    )(side, first, *terms)


def finish_kernel(side_ref, turned_ref, first_ref, second_ref, out_ref):
    turned = turned_ref[side_ref[0]]
    left = side_ref[0] == 0
    for r, straight_ref in enumerate((first_ref, second_ref)):
        near = straight_ref[:LAGS]
        far = jnp.concatenate([turned[:, r, g].reshape(128, 128).T.reshape(8, 16, 128) for g in range(4)], axis=0)
        full = jnp.concatenate([jnp.where(left, far, near), jnp.where(left, near, far)], axis=2)
        out_ref[r] = jnp.swapaxes(full, 0, 1)


def finish(side, turned, straight):
    return pl.pallas_call(
        finish_kernel,
        in_specs=[SMEM] + [pl.BlockSpec(memory_space=pltpu.VMEM)] * 3,
        out_shape=jax.ShapeDtypeStruct((2, 16, LAGS, 256), jnp.float32),
        name="finish",
    )(side, turned, *straight)


def to_partner(mask, value):
    return lax.ppermute(value, "blk", [(b, b ^ mask) for b in range(lax.axis_size("blk"))])


def by_offset(branch, offset, *values):
    count = lax.axis_size("blk")
    return lax.switch(offset - 1, [functools.partial(branch, mask) for mask in range(1, count)], *values)


def swap(value, axis, d):
    return lax.ppermute(value, axis, [(i, i ^ d) for i in range(4)])


def on_device(spectra, masks, plan):
    tables = [jnp.asarray(t) for t in lag_tables()]
    own, rows = whiten(spectra, masks)
    x = ("xh", "xl")
    own = lax.all_gather(own, x, axis=0, tiled=False)
    side = lax.axis_index("xh") ^ parity(chooser(plan[0, 0], plan[1, 0]) & lax.axis_index("blk"))
    place = jnp.stack([lax.axis_index("zh"), lax.axis_index(x), side])
    order = lax.optimization_barrier
    theirs = by_offset(to_partner, plan[0, 0], rows)
    first = [theirs] + [swap(theirs[d], x, d) for d in (1, 2, 3)]
    theirs, rows = order((theirs, rows))
    theirs = by_offset(to_partner, plan[1, 0], rows)
    second = [theirs] + [swap(theirs[d], x, d) for d in (1, 2, 3)]

    first, theirs = order((first, theirs))
    early = stack(place * jnp.array([0, 1, 1], jnp.int32), first, own, *tables)
    early = lax.psum_scatter(early, "zh", scatter_dimension=0, tiled=True)[0]
    late = stack(place, second, own, *tables)
    late = [late] + [swap(late[d], "zh", d) for d in (1, 2, 3)]
    straight = [by_offset(to_partner, plan[0, 0], early)]
    late, straight = order((late, straight))
    sums, turned = pack(side[None], early, late)
    turned = turned.reshape(16, 2, 4, 16, 128)
    turned = lax.all_to_all(turned, ("xh", "xl", "zh"), split_axis=0, concat_axis=0, tiled=True)
    straight.append(by_offset(to_partner, plan[1, 0], sums))
    return finish(side[None], turned.reshape(2, 8, 2, 4, 16, 128), straight)


def solution(mesh):
    fine = Mesh(mesh.devices.reshape(16, 2, 2, 4), ("blk", "xh", "xl", "zh"))
    return jax.shard_map(
        on_device,
        mesh=fine,
        in_specs=(P(None, ("xh", "xl", "zh"), None, "blk"), P(("xh", "xl", "zh"), "blk"), P()),
        out_specs=P(None, ("blk", "xh", "xl", "zh"), None, None),
        check_vma=False,
    )
```

```python
import functools
import math

import jax
import jax.numpy as jnp
import ml_dtypes
import numpy as np
from jax import lax
from jax.experimental import pallas as pl
from jax.experimental.pallas import tpu as pltpu
from jax.sharding import Mesh
from jax.sharding import PartitionSpec as P

LAGS = 32
BINS = 192
WINDOWS = 64
HALF = BINS // 2
STEP = 16
STEPS = HALF // STEP
EVEN = 18
ODD = 16
SMEM = pl.BlockSpec(memory_space=pltpu.SMEM)


def lag_tables():
    norm = 1.0 / math.sqrt(WINDOWS * BINS)
    bins = np.arange(BINS).reshape(2, STEPS, STEP).transpose(1, 2, 0)
    tables = []
    for turn, lags in ((np.cos, np.arange(EVEN)), (np.sin, np.arange(1, ODD + 1))):
        wave = turn(np.pi * bins[..., None] * lags / BINS) * norm * (lags <= LAGS // 2)
        table = np.einsum("sfhl,jk->sljfhk", wave, np.eye(8))
        table = table.reshape(STEPS, 8 * len(lags), STEP * 2 * 8).astype(np.float32)
        high = table.astype(ml_dtypes.bfloat16)
        low = (table - high.astype(np.float32)).astype(ml_dtypes.bfloat16)
        tables.append(np.concatenate([high, low], axis=1))
    return tables


def halves(value):
    high = value.astype(jnp.bfloat16)
    return high, (value - high.astype(jnp.float32)).astype(jnp.bfloat16)


def chooser(first, second):
    common = first & second
    return jnp.where(common != 0, common & -common, (first & -first) | (second & -second))


def parity(bits):
    bits = bits ^ (bits >> 2)
    return (bits ^ (bits >> 1)) & 1


def whiten_kernel(plan_ref, spectra_ref, masks_ref, own_ref, rows_ref):
    parts, windows, bins, channels = spectra_ref.shape
    flag = parity(chooser(plan_ref[0, 0], plan_ref[1, 0]) & lax.axis_index("blk"))
    place = (2 * lax.axis_index("xh") + lax.axis_index("xl")) ^ (2 - 2 * flag)
    pieces = []
    scales = []
    for w in range(windows):
        a, b = spectra_ref[0, w], spectra_ref[1, w]
        power = jnp.sum(a * a + b * b, axis=0, keepdims=True) * (1.0 / bins)
        scales.append(masks_ref[w : w + 1, :].astype(jnp.float32) * lax.rsqrt(power + 1e-06))
    for p in range(parts):
        for w in range(windows):
            pieces.append(spectra_ref[p, w] * scales[w])
    white = jnp.swapaxes(jnp.stack(pieces, axis=0), 0, 1)
    own_ref[...] = white
    lane = lax.broadcasted_iota(jnp.int32, (HALF, 8, 128), 2)
    for block in range(channels // 128):
        a = white[:HALF, :, block * 128 : (block + 1) * 128]
        b = white[HALF:, :, block * 128 : (block + 1) * 128]
        rows_ref[(2 * block) ^ place] = jnp.where(lane < 64, a, pltpu.roll(b, 64, axis=2))
        rows_ref[(2 * block + 1) ^ place] = jnp.where(lane < 64, pltpu.roll(a, 64, axis=2), b)


def whiten(plan, spectra, masks):
    return pl.pallas_call(
        whiten_kernel,
        in_specs=[SMEM, pl.BlockSpec(memory_space=pltpu.VMEM), pl.BlockSpec(memory_space=pltpu.VMEM)],
        out_shape=(
            jax.ShapeDtypeStruct((BINS, 8, 256), jnp.float32),
            jax.ShapeDtypeStruct((4, HALF, 8, 128), jnp.float32),
        ),
        compiler_params=pltpu.CompilerParams(vmem_limit_bytes=32 * 2**20),
        name="whiten",
    )(plan, spectra, masks)


def stack_kernel(place_ref, own_rows_ref, *refs):
    rows_refs, own_refs = refs[:3], refs[3:7]
    cos_ref, sin_ref, out_ref, prod_ref, even_ref, odd_ref = refs[7:]
    step = pl.program_id(0)
    sign = jnp.where(lax.broadcasted_iota(jnp.int32, (4, 8, 128), 1) < 4, 1.0, -1.0)
    dot = functools.partial(jnp.dot, preferred_element_type=jnp.float32)

    def one_low(f, _):
        p = jnp.concatenate([own_rows_ref[0, f]] + [ref[f] for ref in rows_refs], axis=0)
        lh, ll = halves(p)
        left = jnp.concatenate([lh, lh, ll], axis=0).T
        for h in range(2):
            o = jnp.stack([ref[0, h, f] for ref in own_refs], axis=0)
            q = pltpu.roll(o, 4, axis=1) * sign
            rh, rl = halves(jnp.concatenate([o.reshape(32, 128), q.reshape(32, 128)], axis=1))
            right = jnp.concatenate([rh, rl, rh], axis=0)
            prod_ref[2 * f + h] = dot(left[64 * h : 64 * h + 64], right)
        return 0

    lax.fori_loop(0, STEP, one_low, 0, unroll=True)

    @pl.when(step == 0)
    def _():
        even_ref[...] = jnp.zeros_like(even_ref)
        odd_ref[...] = jnp.zeros_like(odd_ref)

    for t in range(4):
        for part, table_ref, sum_ref in ((0, cos_ref, even_ref), (1, sin_ref, odd_ref)):
            size = sum_ref.shape[1]
            lanes = slice(128 * part, 128 * part + 128)
            value = jnp.concatenate(
                [prod_ref[:, 8 * t : 8 * t + 8, lanes], prod_ref[:, 32 + 8 * t : 40 + 8 * t, lanes]], axis=2
            ).reshape(STEP * 16, 256)
            vh, vl = halves(value)
            both = dot(table_ref[0], vh)
            sum_ref[t] += both[:size] + both[size:] + dot(table_ref[0, :size], vl)

    @pl.when(step == STEPS - 1)
    def _():
        mid = LAGS // 2
        for t in range(4):
            even = even_ref[t].reshape(EVEN, 8, 256)
            odd = odd_ref[t].reshape(ODD, 8, 256)
            for k in range(2):
                tile = t + 4 * k
                owner = (tile // 2) ^ place_ref[0]
                place = pl.ds(8 * (tile % 2), 8)
                e, o = even[:, :, 128 * k : 128 * k + 128], odd[:, :, 128 * k : 128 * k + 128]
                out_ref[owner, mid, place] = e[0]
                for lag in range(1, mid + 1):
                    out_ref[owner, mid + lag, place] = e[lag] - o[lag - 1]
                    out_ref[owner, mid - lag, place] = e[lag] + o[lag - 1]


def stack(place, rows, own, cos_t, sin_t):
    own = own.reshape(4, 2, HALF, 8, 256)

    def window(d):
        return pl.BlockSpec((1, 2, STEP, 8, 128), lambda s, place: (place[1] ^ d, 0, s, 0, place[2]))

    return pl.pallas_call(
        stack_kernel,
        grid_spec=pltpu.PrefetchScalarGridSpec(
            num_scalar_prefetch=1,
            grid=(STEPS,),
            in_specs=[pl.BlockSpec((1, STEP, 8, 128), lambda s, place: (0, s, 0, 0))]
            + [pl.BlockSpec((STEP, 8, 128), lambda s, place: (s, 0, 0))] * 3
            + [window(d) for d in range(4)]
            + [
                pl.BlockSpec((1,) + cos_t.shape[1:], lambda s, place: (s, 0, 0)),
                pl.BlockSpec((1,) + sin_t.shape[1:], lambda s, place: (s, 0, 0)),
            ],
            out_specs=pl.BlockSpec((4, LAGS + 1, 16, 128), lambda s, place: (0, 0, 0, 0)),
            scratch_shapes=[
                pltpu.VMEM((2 * STEP, 64, 256), jnp.float32),
                pltpu.VMEM((4, 8 * EVEN, 256), jnp.float32),
                pltpu.VMEM((4, 8 * ODD, 256), jnp.float32),
            ],
        ),
        out_shape=jax.ShapeDtypeStruct((4, LAGS + 1, 16, 128), jnp.float32),
        compiler_params=pltpu.CompilerParams(vmem_limit_bytes=32 * 2**20),
        cost_estimate=pl.CostEstimate(flops=8 * 10**9, bytes_accessed=8 * 2**20, transcendentals=0),
        name="stack",
    )(place, *rows, *[own] * 4, cos_t, sin_t)


def pack_kernel(first_ref, own_ref, *refs):
    terms, sums_ref, out_ref = refs[:-2], refs[-2], refs[-1]
    block = lax.broadcasted_iota(jnp.int32, (16, 128), 1) // 16
    total = own_ref[0]
    for ref in terms:
        total = total + ref[...]
    sums_ref[...] = total
    for r, sums in enumerate((first_ref[...], total)):
        for g in range(4):
            found = [None] * 8
            for k in range(8):
                value = sums[LAGS - 8 * g - k]
                for d in range(8):
                    turned = value if d == k else pltpu.roll(value, 16 * ((k - d) % 8), axis=1)
                    found[d] = turned if k == 0 else jnp.where(block == k, turned, found[d])
            for d in range(8):
                out_ref[d, r, g] = found[d]


def pack(first, terms):
    piece = pl.BlockSpec((LAGS + 1, 16, 128), lambda s: (0, 0, 0))
    return pl.pallas_call(
        pack_kernel,
        grid=(1,),
        in_specs=[piece, pl.BlockSpec((1, LAGS + 1, 16, 128), lambda s: (0, 0, 0, 0))] + [piece] * 3,
        out_specs=(piece, pl.BlockSpec((8, 2, 4, 16, 128), lambda s: (0, 0, 0, 0, 0))),
        out_shape=(
            jax.ShapeDtypeStruct((LAGS + 1, 16, 128), jnp.float32),
            jax.ShapeDtypeStruct((8, 2, 4, 16, 128), jnp.float32),
        ),
        cost_estimate=pl.CostEstimate(flops=10**6, bytes_accessed=3 * 2**20, transcendentals=0),
        name="pack",
    )(first, *terms)


def finish_kernel(flags_ref, turned_ref, *refs):
    out_ref = refs[-1]
    left = flags_ref[1] == 0
    for r in range(2):
        near = jnp.where(flags_ref[0] == 0, refs[2 * r + 1][:LAGS], refs[2 * r][:LAGS])
        far = jnp.concatenate(
            [turned_ref[:, r, g].reshape(128, 128).T.reshape(8, 16, 128) for g in range(4)], axis=0
        )
        full = jnp.concatenate([jnp.where(left, far, near), jnp.where(left, near, far)], axis=2)
        out_ref[r] = jnp.swapaxes(full, 0, 1)


def finish(flags, turned, straight):
    return pl.pallas_call(
        finish_kernel,
        in_specs=[SMEM] + [pl.BlockSpec(memory_space=pltpu.VMEM)] * 5,
        out_shape=jax.ShapeDtypeStruct((2, 16, LAGS, 256), jnp.float32),
        name="finish",
    )(flags, turned, *straight)


def to_partner(mask, value):
    return lax.ppermute(value, "blk", [(b, b ^ mask) for b in range(lax.axis_size("blk"))])


def to_owner(mask, value):
    count = lax.axis_size("blk")
    pairs = [(2 * b + x, 2 * (b ^ mask) + (x ^ 1)) for b in range(count) for x in range(2)]
    return to_partner(mask, value), lax.ppermute(value, ("blk", "xh"), pairs)


def by_offset(branch, offset, *values):
    count = lax.axis_size("blk")
    return lax.switch(offset - 1, [functools.partial(branch, mask) for mask in range(1, count)], *values)


def swap(value, axis, d):
    return lax.ppermute(value, axis, [(i, i ^ d) for i in range(4)])


def swaps(value, axis):
    return [value] + [swap(value[d], axis, d) for d in (1, 2, 3)]


def on_device(spectra, masks, plan):
    tables = [jnp.asarray(t) for t in lag_tables()]
    own, rows = whiten(plan, spectra, masks)
    x = ("xh", "xl")
    own = lax.all_gather(own, x, axis=0, tiled=False)
    flag = parity(chooser(plan[0, 0], plan[1, 0]) & lax.axis_index("blk"))
    side = lax.axis_index("xh")
    place = jnp.stack([lax.axis_index("zh"), lax.axis_index(x), side])
    order = lax.optimization_barrier
    theirs = by_offset(to_partner, plan[0, 0], rows)
    first = swaps(theirs, x)
    theirs, rows = order((theirs, rows))
    theirs = by_offset(to_partner, plan[1, 0], rows)

    def stack_beside(first, theirs, place, own, tables):
        place = place * jnp.array([0, 1, 1], jnp.int32)
        return swaps(theirs, x)[1:], stack(place, first, own, *tables)

    def never(first, theirs, place, own, tables):
        return [piece * 0 for piece in first[1:]], jnp.zeros((4, LAGS + 1, 16, 128), jnp.float32)

    second, early = lax.cond(plan[0, 0] > 0, stack_beside, never, first, theirs, place, own, tables)
    early = lax.psum_scatter(early, "zh", scatter_dimension=0, tiled=True)[0]
    late = swaps(stack(place, [theirs] + second, own, *tables), "zh")
    straight = [*by_offset(to_owner, plan[0, 0], early)]
    late, straight = order((late, straight))
    sums, turned = pack(early, late)
    turned = lax.all_to_all(turned, ("xl", "zh"), split_axis=0, concat_axis=0, tiled=True)
    straight += by_offset(to_owner, plan[1, 0], sums)
    return finish(jnp.stack([flag, side ^ flag]), turned, straight)


def solution(mesh):
    fine = Mesh(mesh.devices.reshape(16, 2, 2, 4), ("blk", "xh", "xl", "zh"))
    return jax.shard_map(
        on_device,
        mesh=fine,
        in_specs=(P(None, ("xh", "xl", "zh"), None, "blk"), P(("xh", "xl", "zh"), "blk"), P()),
        out_specs=P(None, ("blk", "xh", "xl", "zh"), None, None),
        check_vma=False,
    )
```

```python
import functools
import math

import jax
import jax.numpy as jnp
import ml_dtypes
import numpy as np
from jax import lax
from jax.experimental import pallas as pl
from jax.experimental.pallas import tpu as pltpu
from jax.sharding import Mesh
from jax.sharding import PartitionSpec as P

LAGS = 32
BINS = 192
WINDOWS = 64
HALF = BINS // 2
STEP = 16
STEPS = HALF // STEP
EVEN = 18
ODD = 16
SMEM = pl.BlockSpec(memory_space=pltpu.SMEM)


def lag_tables():
    norm = 1.0 / math.sqrt(WINDOWS * BINS)
    bins = np.arange(BINS).reshape(2, STEPS, STEP).transpose(1, 2, 0)
    tables = []
    for turn, lags in ((np.cos, np.arange(EVEN)), (np.sin, np.arange(1, ODD + 1))):
        wave = turn(np.pi * bins[..., None] * lags / BINS) * norm * (lags <= LAGS // 2)
        table = np.einsum("sfhl,jk->sljfhk", wave, np.eye(8))
        table = table.reshape(STEPS, 8 * len(lags), STEP * 2 * 8).astype(np.float32)
        high = table.astype(ml_dtypes.bfloat16)
        low = (table - high.astype(np.float32)).astype(ml_dtypes.bfloat16)
        tables.append(np.concatenate([high, low], axis=1))
    return tables


def halves(value):
    high = value.astype(jnp.bfloat16)
    return high, (value - high.astype(jnp.float32)).astype(jnp.bfloat16)


def chooser(first, second):
    common = first & second
    return jnp.where(common != 0, common & -common, (first & -first) | (second & -second))


def parity(bits):
    bits = bits ^ (bits >> 2)
    return (bits ^ (bits >> 1)) & 1


def whiten_kernel(spectra_ref, masks_ref, own_ref, rows_ref):
    parts, windows, bins, channels = spectra_ref.shape
    x = 2 * lax.axis_index("xh") + lax.axis_index("xl")
    pieces = []
    scales = []
    for w in range(windows):
        a, b = spectra_ref[0, w], spectra_ref[1, w]
        power = jnp.sum(a * a + b * b, axis=0, keepdims=True) * (1.0 / bins)
        scales.append(masks_ref[w : w + 1, :].astype(jnp.float32) * lax.rsqrt(power + 1e-06))
    for p in range(parts):
        for w in range(windows):
            pieces.append(spectra_ref[p, w] * scales[w])
    white = jnp.swapaxes(jnp.stack(pieces, axis=0), 0, 1)
    own_ref[...] = white
    lane = lax.broadcasted_iota(jnp.int32, (HALF, 8, 128), 2)
    for block in range(channels // 128):
        a = white[:HALF, :, block * 128 : (block + 1) * 128]
        b = white[HALF:, :, block * 128 : (block + 1) * 128]
        rows_ref[(2 * block) ^ x] = jnp.where(lane < 64, a, pltpu.roll(b, 64, axis=2))
        rows_ref[(2 * block + 1) ^ x] = jnp.where(lane < 64, pltpu.roll(a, 64, axis=2), b)


def whiten(spectra, masks):
    return pl.pallas_call(
        whiten_kernel,
        out_shape=(
            jax.ShapeDtypeStruct((BINS, 8, 256), jnp.float32),
            jax.ShapeDtypeStruct((4, HALF, 8, 128), jnp.float32),
        ),
        compiler_params=pltpu.CompilerParams(vmem_limit_bytes=32 * 2**20),
        name="whiten",
    )(spectra, masks)


def stack_kernel(place_ref, own_rows_ref, *refs):
    rows_refs, own_refs = refs[:3], refs[3:7]
    cos_ref, sin_ref, out_ref, prod_ref, even_ref, odd_ref = refs[7:]
    step = pl.program_id(0)
    sign = jnp.where(lax.broadcasted_iota(jnp.int32, (4, 8, 256), 1) < 4, 1.0, -1.0)
    dot = functools.partial(jnp.dot, preferred_element_type=jnp.float32)

    def one_low(f, _):
        p = jnp.concatenate([own_rows_ref[0, f]] + [ref[f] for ref in rows_refs], axis=0)
        lh, ll = halves(p)
        left = jnp.concatenate([lh, lh, ll], axis=0).T
        for h in range(2):
            o = jnp.stack([ref[0, h, f] for ref in own_refs], axis=0)
            q = pltpu.roll(o, 4, axis=1) * sign
            rh, rl = halves(jnp.concatenate([o.reshape(32, 256), q.reshape(32, 256)], axis=1))
            right = jnp.concatenate([rh, rl, rh], axis=0)
            prod_ref[2 * f + h] = dot(left[64 * h : 64 * h + 64], right)
        return 0

    lax.fori_loop(0, STEP, one_low, 0, unroll=True)

    @pl.when(step == 0)
    def _():
        even_ref[...] = jnp.zeros_like(even_ref)
        odd_ref[...] = jnp.zeros_like(odd_ref)

    for t in range(8):
        for part, table_ref, sum_ref in ((0, cos_ref, even_ref), (1, sin_ref, odd_ref)):
            size = sum_ref.shape[1]
            value = prod_ref[:, 8 * t : 8 * t + 8, 256 * part : 256 * part + 256].reshape(STEP * 16, 256)
            vh, vl = halves(value)
            both = dot(table_ref[0], vh)
            sum_ref[t] += both[:size] + both[size:] + dot(table_ref[0, :size], vl)

    @pl.when(step == STEPS - 1)
    def _():
        mid = LAGS // 2
        for t in range(8):
            e = even_ref[t].reshape(EVEN, 8, 256)
            o = odd_ref[t].reshape(ODD, 8, 256)
            place = pl.ds(8 * (t % 2), 8)
            out_ref[t // 2, mid, place] = e[0]
            for lag in range(1, mid + 1):
                out_ref[t // 2, mid + lag, place] = e[lag] - o[lag - 1]
                out_ref[t // 2, mid - lag, place] = e[lag] + o[lag - 1]


def stack(place, rows, own, cos_t, sin_t):
    own = own.reshape(4, 2, HALF, 8, 256)

    def window(d):
        return pl.BlockSpec((1, 2, STEP, 8, 256), lambda s, place: (place[0] ^ d, 0, s, 0, 0))

    return pl.pallas_call(
        stack_kernel,
        grid_spec=pltpu.PrefetchScalarGridSpec(
            num_scalar_prefetch=1,
            grid=(STEPS,),
            in_specs=[pl.BlockSpec((1, STEP, 8, 128), lambda s, place: (0, s, 0, 0))]
            + [pl.BlockSpec((STEP, 8, 128), lambda s, place: (s, 0, 0))] * 3
            + [window(d) for d in range(4)]
            + [
                pl.BlockSpec((1,) + cos_t.shape[1:], lambda s, place: (s, 0, 0)),
                pl.BlockSpec((1,) + sin_t.shape[1:], lambda s, place: (s, 0, 0)),
            ],
            out_specs=pl.BlockSpec((4, LAGS + 1, 16, 256), lambda s, place: (0, 0, 0, 0)),
            scratch_shapes=[
                pltpu.VMEM((2 * STEP, 64, 512), jnp.float32),
                pltpu.VMEM((8, 8 * EVEN, 256), jnp.float32),
                pltpu.VMEM((8, 8 * ODD, 256), jnp.float32),
            ],
        ),
        out_shape=jax.ShapeDtypeStruct((4, LAGS + 1, 16, 256), jnp.float32),
        compiler_params=pltpu.CompilerParams(vmem_limit_bytes=40 * 2**20),
        cost_estimate=pl.CostEstimate(flops=14 * 10**9, bytes_accessed=12 * 2**20, transcendentals=0),
        name="stack",
    )(place, *rows, *[own] * 4, cos_t, sin_t)


def pack_kernel(sums_ref, out_ref):
    block = lax.broadcasted_iota(jnp.int32, (16, 128), 1) // 16
    for half in range(2):
        for g in range(4):
            found = [None] * 8
            for k in range(8):
                value = sums_ref[LAGS - 8 * g - k, :, 128 * half : 128 * half + 128]
                for d in range(8):
                    turned = value if d == k else pltpu.roll(value, 16 * ((k - d) % 8), axis=1)
                    found[d] = turned if k == 0 else jnp.where(block == k, turned, found[d])
            for d in range(8):
                out_ref[8 * half + d, g] = found[d]


def pack(sums):
    return pl.pallas_call(
        pack_kernel,
        out_shape=jax.ShapeDtypeStruct((16, 4, 16, 128), jnp.float32),
        cost_estimate=pl.CostEstimate(flops=10**6, bytes_accessed=2 * 2**20, transcendentals=0),
        name="pack",
    )(sums)


def finish_kernel(flags_ref, turned_ref, low_ref, high_ref, out_ref):
    own = jnp.concatenate([turned_ref[:, g].reshape(256, 128).T.reshape(8, 16, 256) for g in range(4)], axis=0)
    out_ref[flags_ref[1]] = jnp.swapaxes(own, 0, 1)
    sent = jnp.where(flags_ref[0] == 1, low_ref[:LAGS], high_ref[:LAGS])
    out_ref[1 - flags_ref[1]] = jnp.swapaxes(sent, 0, 1)


def finish(flags, turned, low, high):
    return pl.pallas_call(
        finish_kernel,
        in_specs=[SMEM] + [pl.BlockSpec(memory_space=pltpu.VMEM)] * 3,
        out_shape=jax.ShapeDtypeStruct((2, 16, LAGS, 256), jnp.float32),
        name="finish",
    )(flags, turned, low, high)


def to_partner(mask, value):
    return lax.ppermute(value, "blk", [(b, b ^ mask) for b in range(lax.axis_size("blk"))])


def by_offset(branch, offset, *values):
    count = lax.axis_size("blk")
    return lax.switch(offset - 1, [functools.partial(branch, mask) for mask in range(1, count)], *values)


def fetch(low, high, value):
    common = low & high
    bits = common & -common if common else (low & -low) | (high & -high)
    pairs = [(b ^ (high if (b & bits).bit_count() & 1 else low), b) for b in range(lax.axis_size("blk"))]
    return lax.ppermute(value, "blk", pairs)


def by_offsets(low, high, value):
    count = lax.axis_size("blk")
    branches = [functools.partial(fetch, a, c) for c in range(2, count) for a in range(1, c)]
    return lax.switch((high - 1) * (high - 2) // 2 + low - 1, branches, value)


def swap(value, axis, d):
    return lax.ppermute(value, axis, [(i, i ^ d) for i in range(4)])


def on_device(spectra, masks, plan):
    tables = [jnp.asarray(t) for t in lag_tables()]
    own, rows = whiten(spectra, masks)
    x = ("xh", "xl")
    own = lax.all_gather(own, x, axis=0, tiled=False)
    low, high = jnp.minimum(plan[0, 0], plan[1, 0]), jnp.maximum(plan[0, 0], plan[1, 0])
    flag = parity(chooser(low, high) & lax.axis_index("blk"))
    swapped = (plan[0, 0] > plan[1, 0]).astype(jnp.int32)
    theirs = by_offsets(low, high, rows)
    theirs = [theirs] + [swap(theirs[d], x, d) for d in (1, 2, 3)]
    sums = stack(lax.axis_index(x)[None], theirs, own, *tables)
    sums = lax.psum_scatter(sums, "zh", scatter_dimension=0, tiled=True)[0]
    turned = lax.all_to_all(pack(sums), ("xh", "xl", "zh"), split_axis=0, concat_axis=0, tiled=True)
    back = [by_offset(to_partner, offset, sums) for offset in (low, high)]
    return finish(jnp.stack([flag, flag ^ swapped]), turned, *back)


def solution(mesh):
    fine = Mesh(mesh.devices.reshape(16, 2, 2, 4), ("blk", "xh", "xl", "zh"))
    return jax.shard_map(
        on_device,
        mesh=fine,
        in_specs=(P(None, ("xh", "xl", "zh"), None, "blk"), P(("xh", "xl", "zh"), "blk"), P()),
        out_specs=P(None, ("blk", "xh", "xl", "zh"), None, None),
        check_vma=False,
    )
```

```python
import functools
import math

import jax
import jax.numpy as jnp
import ml_dtypes
import numpy as np
from jax import lax
from jax.experimental import pallas as pl
from jax.experimental.pallas import tpu as pltpu
from jax.sharding import Mesh
from jax.sharding import PartitionSpec as P

LAGS = 32
BINS = 192
WINDOWS = 64
HALF = BINS // 2
STEP = 16
STEPS = HALF // STEP
EVEN = 18
ODD = 16
SMEM = pl.BlockSpec(memory_space=pltpu.SMEM)


def lag_tables():
    norm = 1.0 / math.sqrt(WINDOWS * BINS)
    bins = np.arange(BINS).reshape(2, STEPS, STEP).transpose(1, 2, 0)
    tables = []
    for turn, lags in ((np.cos, np.arange(EVEN)), (np.sin, np.arange(1, ODD + 1))):
        wave = turn(np.pi * bins[..., None] * lags / BINS) * norm * (lags <= LAGS // 2)
        table = np.einsum("sfhl,jk->sljfhk", wave, np.eye(8))
        table = table.reshape(STEPS, 8 * len(lags), STEP * 2 * 8).astype(np.float32)
        high = table.astype(ml_dtypes.bfloat16)
        low = (table - high.astype(np.float32)).astype(ml_dtypes.bfloat16)
        tables.append(np.concatenate([high, low], axis=1))
    return tables


def halves(value):
    high = value.astype(jnp.bfloat16)
    return high, (value - high.astype(jnp.float32)).astype(jnp.bfloat16)


def chooser(first, second):
    common = first & second
    return jnp.where(common != 0, common & -common, (first & -first) | (second & -second))


def parity(bits):
    bits = bits ^ (bits >> 2)
    return (bits ^ (bits >> 1)) & 1


def whiten_kernel(spectra_ref, masks_ref, own_ref, rows_ref):
    parts, windows, bins, channels = spectra_ref.shape
    x = 2 * lax.axis_index("xh") + lax.axis_index("xl")
    pieces = []
    scales = []
    for w in range(windows):
        a, b = spectra_ref[0, w], spectra_ref[1, w]
        power = jnp.sum(a * a + b * b, axis=0, keepdims=True) * (1.0 / bins)
        scales.append(masks_ref[w : w + 1, :].astype(jnp.float32) * lax.rsqrt(power + 1e-06))
    for p in range(parts):
        for w in range(windows):
            pieces.append(spectra_ref[p, w] * scales[w])
    white = jnp.swapaxes(jnp.stack(pieces, axis=0), 0, 1)
    own_ref[...] = white
    lane = lax.broadcasted_iota(jnp.int32, (HALF, 8, 128), 2)
    for block in range(channels // 128):
        a = white[:HALF, :, block * 128 : (block + 1) * 128]
        b = white[HALF:, :, block * 128 : (block + 1) * 128]
        rows_ref[(2 * block) ^ x] = jnp.where(lane < 64, a, pltpu.roll(b, 64, axis=2))
        rows_ref[(2 * block + 1) ^ x] = jnp.where(lane < 64, pltpu.roll(a, 64, axis=2), b)


def whiten(spectra, masks):
    return pl.pallas_call(
        whiten_kernel,
        out_shape=(
            jax.ShapeDtypeStruct((BINS, 8, 256), jnp.float32),
            jax.ShapeDtypeStruct((4, HALF, 8, 128), jnp.float32),
        ),
        compiler_params=pltpu.CompilerParams(vmem_limit_bytes=32 * 2**20),
        name="whiten",
    )(spectra, masks)


def stack_kernel(place_ref, high_ref, own_rows_ref, *refs):
    rows_refs, own_refs = refs[:3], refs[3:7]
    cos_ref, sin_ref, out_ref, prod_ref, even_ref, odd_ref = refs[7:]
    take_high = place_ref[1] == 1
    step = pl.program_id(0)
    sign = jnp.where(lax.broadcasted_iota(jnp.int32, (4, 8, 256), 1) < 4, 1.0, -1.0)
    dot = functools.partial(jnp.dot, preferred_element_type=jnp.float32)

    def one_low(f, _):
        p = jnp.concatenate([own_rows_ref[0, f]] + [ref[f] for ref in rows_refs], axis=0)
        p = jnp.where(take_high, high_ref[:, f].reshape(32, 128), p)
        lh, ll = halves(p)
        left = jnp.concatenate([lh, lh, ll], axis=0).T
        for h in range(2):
            o = jnp.stack([ref[0, h, f] for ref in own_refs], axis=0)
            q = pltpu.roll(o, 4, axis=1) * sign
            rh, rl = halves(jnp.concatenate([o.reshape(32, 256), q.reshape(32, 256)], axis=1))
            right = jnp.concatenate([rh, rl, rh], axis=0)
            prod_ref[2 * f + h] = dot(left[64 * h : 64 * h + 64], right)
        return 0

    lax.fori_loop(0, STEP, one_low, 0, unroll=True)

    @pl.when(step == 0)
    def _():
        even_ref[...] = jnp.zeros_like(even_ref)
        odd_ref[...] = jnp.zeros_like(odd_ref)

    for t in range(8):
        for part, table_ref, sum_ref in ((0, cos_ref, even_ref), (1, sin_ref, odd_ref)):
            size = sum_ref.shape[1]
            value = prod_ref[:, 8 * t : 8 * t + 8, 256 * part : 256 * part + 256].reshape(STEP * 16, 256)
            vh, vl = halves(value)
            both = dot(table_ref[0], vh)
            sum_ref[t] += both[:size] + both[size:] + dot(table_ref[0, :size], vl)

    @pl.when(step == STEPS - 1)
    def _():
        mid = LAGS // 2
        for t in range(8):
            e = even_ref[t].reshape(EVEN, 8, 256)
            o = odd_ref[t].reshape(ODD, 8, 256)
            place = pl.ds(8 * (t % 2), 8)
            out_ref[t // 2, mid, place] = e[0]
            for lag in range(1, mid + 1):
                out_ref[t // 2, mid + lag, place] = e[lag] - o[lag - 1]
                out_ref[t // 2, mid - lag, place] = e[lag] + o[lag - 1]


def stack(place, low_rows, high_rows, own, cos_t, sin_t):
    own = own.reshape(4, 2, HALF, 8, 256)

    def window(d):
        return pl.BlockSpec((1, 2, STEP, 8, 256), lambda s, place: (place[0] ^ d, 0, s, 0, 0))

    return pl.pallas_call(
        stack_kernel,
        grid_spec=pltpu.PrefetchScalarGridSpec(
            num_scalar_prefetch=1,
            grid=(STEPS,),
            in_specs=[pl.BlockSpec((4, STEP, 8, 128), lambda s, place: (0, s, 0, 0))]
            + [pl.BlockSpec((1, STEP, 8, 128), lambda s, place: (0, s, 0, 0))]
            + [pl.BlockSpec((STEP, 8, 128), lambda s, place: (s, 0, 0))] * 3
            + [window(d) for d in range(4)]
            + [
                pl.BlockSpec((1,) + cos_t.shape[1:], lambda s, place: (s, 0, 0)),
                pl.BlockSpec((1,) + sin_t.shape[1:], lambda s, place: (s, 0, 0)),
            ],
            out_specs=pl.BlockSpec((4, LAGS + 1, 16, 256), lambda s, place: (0, 0, 0, 0)),
            scratch_shapes=[
                pltpu.VMEM((2 * STEP, 64, 512), jnp.float32),
                pltpu.VMEM((8, 8 * EVEN, 256), jnp.float32),
                pltpu.VMEM((8, 8 * ODD, 256), jnp.float32),
            ],
        ),
        out_shape=jax.ShapeDtypeStruct((4, LAGS + 1, 16, 256), jnp.float32),
        compiler_params=pltpu.CompilerParams(vmem_limit_bytes=40 * 2**20),
        cost_estimate=pl.CostEstimate(flops=14 * 10**9, bytes_accessed=12 * 2**20, transcendentals=0),
        name="stack",
    )(place, high_rows, *low_rows, *[own] * 4, cos_t, sin_t)


def pack_kernel(sums_ref, out_ref):
    block = lax.broadcasted_iota(jnp.int32, (16, 128), 1) // 16
    for half in range(2):
        for g in range(4):
            found = [None] * 8
            for k in range(8):
                value = sums_ref[LAGS - 8 * g - k, :, 128 * half : 128 * half + 128]
                for d in range(8):
                    turned = value if d == k else pltpu.roll(value, 16 * ((k - d) % 8), axis=1)
                    found[d] = turned if k == 0 else jnp.where(block == k, turned, found[d])
            for d in range(8):
                out_ref[8 * half + d, g] = found[d]


def pack(sums):
    return pl.pallas_call(
        pack_kernel,
        out_shape=jax.ShapeDtypeStruct((16, 4, 16, 128), jnp.float32),
        cost_estimate=pl.CostEstimate(flops=10**6, bytes_accessed=2 * 2**20, transcendentals=0),
        name="pack",
    )(sums)


def finish_kernel(flags_ref, turned_ref, low_ref, high_ref, out_ref):
    own = jnp.concatenate([turned_ref[:, g].reshape(256, 128).T.reshape(8, 16, 256) for g in range(4)], axis=0)
    out_ref[flags_ref[1]] = jnp.swapaxes(own, 0, 1)
    sent = jnp.where(flags_ref[0] == 1, low_ref[:LAGS], high_ref[:LAGS])
    out_ref[1 - flags_ref[1]] = jnp.swapaxes(sent, 0, 1)


def finish(flags, turned, low, high):
    return pl.pallas_call(
        finish_kernel,
        in_specs=[SMEM] + [pl.BlockSpec(memory_space=pltpu.VMEM)] * 3,
        out_shape=jax.ShapeDtypeStruct((2, 16, LAGS, 256), jnp.float32),
        name="finish",
    )(flags, turned, low, high)


def to_partner(mask, value):
    return lax.ppermute(value, "blk", [(b, b ^ mask) for b in range(lax.axis_size("blk"))])


def by_offset(branch, offset, *values):
    count = lax.axis_size("blk")
    return lax.switch(offset - 1, [functools.partial(branch, mask) for mask in range(1, count)], *values)


def swap(value, axis, d):
    return lax.ppermute(value, axis, [(i, i ^ d) for i in range(4)])


def on_device(spectra, masks, plan):
    tables = [jnp.asarray(t) for t in lag_tables()]
    own, rows = whiten(spectra, masks)
    x = ("xh", "xl")
    own = lax.all_gather(own, x, axis=0, tiled=False)
    low, high = jnp.minimum(plan[0, 0], plan[1, 0]), jnp.maximum(plan[0, 0], plan[1, 0])
    flag = parity(chooser(low, high) & lax.axis_index("blk"))
    swapped = (plan[0, 0] > plan[1, 0]).astype(jnp.int32)
    order = lax.optimization_barrier
    gathered = jnp.stack([rows[0]] + [swap(rows[d], x, d) for d in (1, 2, 3)], axis=0)
    theirs = by_offset(to_partner, low, rows)
    gathered, theirs = order((gathered, theirs))
    low_rows = [theirs] + [swap(theirs[d], x, d) for d in (1, 2, 3)]
    high_rows = by_offset(to_partner, high, gathered)
    place = jnp.stack([lax.axis_index(x), flag])
    sums = stack(place, low_rows, high_rows, own, *tables)
    sums = lax.psum_scatter(sums, "zh", scatter_dimension=0, tiled=True)[0]
    low_back = by_offset(to_partner, low, sums)
    sums, low_back = order((sums, low_back))
    turned = lax.all_to_all(pack(sums), ("xh", "xl", "zh"), split_axis=0, concat_axis=0, tiled=True)
    high_back = by_offset(to_partner, high, sums)
    return finish(jnp.stack([flag, flag ^ swapped]), turned, low_back, high_back)


def solution(mesh):
    fine = Mesh(mesh.devices.reshape(16, 2, 2, 4), ("blk", "xh", "xl", "zh"))
    return jax.shard_map(
        on_device,
        mesh=fine,
        in_specs=(P(None, ("xh", "xl", "zh"), None, "blk"), P(("xh", "xl", "zh"), "blk"), P()),
        out_specs=P(None, ("blk", "xh", "xl", "zh"), None, None),
        check_vma=False,
    )
```

```python
import functools
import math

import jax
import jax.numpy as jnp
import ml_dtypes
import numpy as np
from jax import lax
from jax.experimental import pallas as pl
from jax.experimental.pallas import tpu as pltpu
from jax.sharding import Mesh
from jax.sharding import PartitionSpec as P

LAGS = 32
BINS = 192
WINDOWS = 64
HALF = BINS // 2
STEP = 16
STEPS = HALF // STEP
EVEN = 18
ODD = 16
SMEM = pl.BlockSpec(memory_space=pltpu.SMEM)


def lag_tables():
    norm = 1.0 / math.sqrt(WINDOWS * BINS)
    bins = np.arange(BINS).reshape(2, STEPS, STEP).transpose(1, 2, 0)
    tables = []
    for turn, lags in ((np.cos, np.arange(EVEN)), (np.sin, np.arange(1, ODD + 1))):
        wave = turn(np.pi * bins[..., None] * lags / BINS) * norm * (lags <= LAGS // 2)
        table = np.einsum("sfhl,jk->sljfhk", wave, np.eye(8))
        table = table.reshape(STEPS, 8 * len(lags), STEP * 2 * 8).astype(np.float32)
        high = table.astype(ml_dtypes.bfloat16)
        low = (table - high.astype(np.float32)).astype(ml_dtypes.bfloat16)
        tables.append(np.concatenate([high, low], axis=1))
    return tables


def halves(value):
    high = value.astype(jnp.bfloat16)
    return high, (value - high.astype(jnp.float32)).astype(jnp.bfloat16)


def chooser(first, second):
    common = first & second
    return jnp.where(common != 0, common & -common, (first & -first) | (second & -second))


def parity(bits):
    bits = bits ^ (bits >> 2)
    return (bits ^ (bits >> 1)) & 1


def whiten_kernel(spectra_ref, masks_ref, own_ref, rows_ref):
    parts, windows, bins, channels = spectra_ref.shape
    pieces = []
    scales = []
    for w in range(windows):
        a, b = spectra_ref[0, w], spectra_ref[1, w]
        power = jnp.sum(a * a + b * b, axis=0, keepdims=True) * (1.0 / bins)
        scales.append(masks_ref[w : w + 1, :].astype(jnp.float32) * lax.rsqrt(power + 1e-06))
    for p in range(parts):
        for w in range(windows):
            pieces.append(spectra_ref[p, w] * scales[w])
    white = jnp.swapaxes(jnp.stack(pieces, axis=0), 0, 1)
    own_ref[...] = white
    lane = lax.broadcasted_iota(jnp.int32, (HALF, 8, 128), 2)
    for block in range(channels // 128):
        a = white[:HALF, :, block * 128 : (block + 1) * 128]
        b = white[HALF:, :, block * 128 : (block + 1) * 128]
        rows_ref[2 * block] = jnp.where(lane < 64, a, pltpu.roll(b, 64, axis=2))
        rows_ref[2 * block + 1] = jnp.where(lane < 64, pltpu.roll(a, 64, axis=2), b)


def whiten(spectra, masks):
    return pl.pallas_call(
        whiten_kernel,
        out_shape=(
            jax.ShapeDtypeStruct((BINS, 8, 256), jnp.float32),
            jax.ShapeDtypeStruct((4, HALF, 8, 128), jnp.float32),
        ),
        compiler_params=pltpu.CompilerParams(vmem_limit_bytes=32 * 2**20),
        name="whiten",
    )(spectra, masks)


def stack_kernel(
    flag_ref, low_ref, high_ref, own_ref, cos_ref, sin_ref, out_ref, prod_ref, even_ref, odd_ref
):
    take_high = flag_ref[0] == 1
    step = pl.program_id(0)
    sign = jnp.where(lax.broadcasted_iota(jnp.int32, (4, 8, 256), 1) < 4, 1.0, -1.0)
    dot = functools.partial(jnp.dot, preferred_element_type=jnp.float32)

    def one_low(f, _):
        p = jnp.where(take_high, high_ref[:, f].reshape(32, 128), low_ref[:, f].reshape(32, 128))
        lh, ll = halves(p)
        left = jnp.concatenate([lh, lh, ll], axis=0).T
        for h in range(2):
            o = own_ref[:, h, f]
            q = pltpu.roll(o, 4, axis=1) * sign
            rh, rl = halves(jnp.concatenate([o.reshape(32, 256), q.reshape(32, 256)], axis=1))
            right = jnp.concatenate([rh, rl, rh], axis=0)
            prod_ref[2 * f + h] = dot(left[64 * h : 64 * h + 64], right)
        return 0

    lax.fori_loop(0, STEP, one_low, 0, unroll=True)

    @pl.when(step == 0)
    def _():
        even_ref[...] = jnp.zeros_like(even_ref)
        odd_ref[...] = jnp.zeros_like(odd_ref)

    for t in range(8):
        for part, table_ref, sum_ref in ((0, cos_ref, even_ref), (1, sin_ref, odd_ref)):
            size = sum_ref.shape[1]
            value = prod_ref[:, 8 * t : 8 * t + 8, 256 * part : 256 * part + 256].reshape(STEP * 16, 256)
            vh, vl = halves(value)
            both = dot(table_ref[0], vh)
            sum_ref[t] += both[:size] + both[size:] + dot(table_ref[0, :size], vl)

    @pl.when(step == STEPS - 1)
    def _():
        mid = LAGS // 2
        for t in range(8):
            e = even_ref[t].reshape(EVEN, 8, 256)
            o = odd_ref[t].reshape(ODD, 8, 256)
            place = pl.ds(8 * (t % 2), 8)
            out_ref[t // 2, mid, place] = e[0]
            for lag in range(1, mid + 1):
                out_ref[t // 2, mid + lag, place] = e[lag] - o[lag - 1]
                out_ref[t // 2, mid - lag, place] = e[lag] + o[lag - 1]


def stack(flag, low_rows, high_rows, own, cos_t, sin_t):
    own = own.reshape(4, 2, HALF, 8, 256)
    return pl.pallas_call(
        stack_kernel,
        grid_spec=pltpu.PrefetchScalarGridSpec(
            num_scalar_prefetch=1,
            grid=(STEPS,),
            in_specs=[pl.BlockSpec((4, STEP, 8, 128), lambda s, flag: (0, s, 0, 0))] * 2
            + [pl.BlockSpec((4, 2, STEP, 8, 256), lambda s, flag: (0, 0, s, 0, 0))]
            + [
                pl.BlockSpec((1,) + cos_t.shape[1:], lambda s, flag: (s, 0, 0)),
                pl.BlockSpec((1,) + sin_t.shape[1:], lambda s, flag: (s, 0, 0)),
            ],
            out_specs=pl.BlockSpec((4, LAGS + 1, 16, 256), lambda s, flag: (0, 0, 0, 0)),
            scratch_shapes=[
                pltpu.VMEM((2 * STEP, 64, 512), jnp.float32),
                pltpu.VMEM((8, 8 * EVEN, 256), jnp.float32),
                pltpu.VMEM((8, 8 * ODD, 256), jnp.float32),
            ],
        ),
        out_shape=jax.ShapeDtypeStruct((4, LAGS + 1, 16, 256), jnp.float32),
        compiler_params=pltpu.CompilerParams(vmem_limit_bytes=40 * 2**20),
        cost_estimate=pl.CostEstimate(flops=14 * 10**9, bytes_accessed=12 * 2**20, transcendentals=0),
        name="stack",
    )(flag, low_rows, high_rows, own, cos_t, sin_t)


def pack_kernel(sums_ref, out_ref):
    block = lax.broadcasted_iota(jnp.int32, (16, 128), 1) // 16
    for half in range(2):
        for g in range(4):
            found = [None] * 8
            for k in range(8):
                value = sums_ref[LAGS - 8 * g - k, :, 128 * half : 128 * half + 128]
                for d in range(8):
                    turned = value if d == k else pltpu.roll(value, 16 * ((k - d) % 8), axis=1)
                    found[d] = turned if k == 0 else jnp.where(block == k, turned, found[d])
            for d in range(8):
                out_ref[8 * half + d, g] = found[d]


def pack(sums):
    return pl.pallas_call(
        pack_kernel,
        out_shape=jax.ShapeDtypeStruct((16, 4, 16, 128), jnp.float32),
        cost_estimate=pl.CostEstimate(flops=10**6, bytes_accessed=2 * 2**20, transcendentals=0),
        name="pack",
    )(sums)


def finish_kernel(flags_ref, turned_ref, low_ref, high_ref, out_ref):
    own = jnp.concatenate([turned_ref[:, g].reshape(256, 128).T.reshape(8, 16, 256) for g in range(4)], axis=0)
    out_ref[flags_ref[1]] = jnp.swapaxes(own, 0, 1)
    sent = jnp.where(flags_ref[0] == 1, low_ref[:LAGS], high_ref[:LAGS])
    out_ref[1 - flags_ref[1]] = jnp.swapaxes(sent, 0, 1)


def finish(flags, turned, low, high):
    return pl.pallas_call(
        finish_kernel,
        in_specs=[SMEM] + [pl.BlockSpec(memory_space=pltpu.VMEM)] * 3,
        out_shape=jax.ShapeDtypeStruct((2, 16, LAGS, 256), jnp.float32),
        name="finish",
    )(flags, turned, low, high)


def to_partner(mask, value):
    return lax.ppermute(value, "blk", [(b, b ^ mask) for b in range(lax.axis_size("blk"))])


def by_offset(branch, offset, *values):
    count = lax.axis_size("blk")
    return lax.switch(offset - 1, [functools.partial(branch, mask) for mask in range(1, count)], *values)


def spread(value, axis):
    return lax.all_to_all(value, axis, split_axis=0, concat_axis=0, tiled=True)


def on_device(spectra, masks, plan):
    tables = [jnp.asarray(t) for t in lag_tables()]
    own, rows = whiten(spectra, masks)
    x = ("xh", "xl")
    own = lax.all_gather(own, x, axis=0, tiled=False)
    low, high = jnp.minimum(plan[0, 0], plan[1, 0]), jnp.maximum(plan[0, 0], plan[1, 0])
    flag = parity(chooser(low, high) & lax.axis_index("blk"))
    swapped = (plan[0, 0] > plan[1, 0]).astype(jnp.int32)
    order = lax.optimization_barrier
    gathered = spread(rows, x)
    theirs = by_offset(to_partner, low, rows)
    gathered, theirs = order((gathered, theirs))
    low_rows = spread(theirs, x)
    high_rows = by_offset(to_partner, high, gathered)
    sums = stack(flag[None], low_rows, high_rows, own, *tables)
    sums = lax.psum_scatter(sums, "zh", scatter_dimension=0, tiled=True)[0]
    low_back = by_offset(to_partner, low, sums)
    sums, low_back = order((sums, low_back))
    turned = spread(pack(sums), ("xh", "xl", "zh"))
    high_back = by_offset(to_partner, high, sums)
    return finish(jnp.stack([flag, flag ^ swapped]), turned, low_back, high_back)


def solution(mesh):
    fine = Mesh(mesh.devices.reshape(16, 2, 2, 4), ("blk", "xh", "xl", "zh"))
    return jax.shard_map(
        on_device,
        mesh=fine,
        in_specs=(P(None, ("xh", "xl", "zh"), None, "blk"), P(("xh", "xl", "zh"), "blk"), P()),
        out_specs=P(None, ("blk", "xh", "xl", "zh"), None, None),
        check_vma=False,
    )
```

```python
import functools
import math

import jax
import jax.numpy as jnp
import ml_dtypes
import numpy as np
from jax import lax
from jax.experimental import pallas as pl
from jax.experimental.pallas import tpu as pltpu
from jax.sharding import Mesh
from jax.sharding import PartitionSpec as P

LAGS = 32
BINS = 192
WINDOWS = 64
HALF = BINS // 2
STEP = 16
STEPS = HALF // STEP
EVEN = 18
ODD = 16
SMEM = pl.BlockSpec(memory_space=pltpu.SMEM)


def lag_tables():
    norm = 1.0 / math.sqrt(WINDOWS * BINS)
    bins = np.arange(BINS).reshape(2, STEPS, STEP).transpose(1, 2, 0)
    tables = []
    for turn, lags in ((np.cos, np.arange(EVEN)), (np.sin, np.arange(1, ODD + 1))):
        wave = turn(np.pi * bins[..., None] * lags / BINS) * norm * (lags <= LAGS // 2)
        table = np.einsum("sfhl,jk->sljfhk", wave, np.eye(8))
        table = table.reshape(STEPS, 8 * len(lags), STEP * 2 * 8).astype(np.float32)
        high = table.astype(ml_dtypes.bfloat16)
        low = (table - high.astype(np.float32)).astype(ml_dtypes.bfloat16)
        tables.append(np.concatenate([high, low], axis=1))
    return tables


def halves(value):
    high = value.astype(jnp.bfloat16)
    return high, (value - high.astype(jnp.float32)).astype(jnp.bfloat16)


def whiten_kernel(spectra_ref, masks_ref, own_ref, rows_ref):
    parts, windows, bins, channels = spectra_ref.shape
    pieces = []
    scales = []
    for w in range(windows):
        a, b = spectra_ref[0, w], spectra_ref[1, w]
        power = jnp.sum(a * a + b * b, axis=0, keepdims=True) * (1.0 / bins)
        scales.append(masks_ref[w : w + 1, :].astype(jnp.float32) * lax.rsqrt(power + 1e-06))
    for p in range(parts):
        for w in range(windows):
            pieces.append(spectra_ref[p, w] * scales[w])
    white = jnp.swapaxes(jnp.stack(pieces, axis=0), 0, 1)
    own_ref[...] = white
    lane = lax.broadcasted_iota(jnp.int32, (HALF, 8, 128), 2)
    for block in range(channels // 128):
        a = white[:HALF, :, block * 128 : (block + 1) * 128]
        b = white[HALF:, :, block * 128 : (block + 1) * 128]
        rows_ref[2 * block] = jnp.where(lane < 64, a, pltpu.roll(b, 64, axis=2))
        rows_ref[2 * block + 1] = jnp.where(lane < 64, pltpu.roll(a, 64, axis=2), b)


def whiten(spectra, masks):
    return pl.pallas_call(
        whiten_kernel,
        out_shape=(
            jax.ShapeDtypeStruct((BINS, 8, 256), jnp.float32),
            jax.ShapeDtypeStruct((4, HALF, 8, 128), jnp.float32),
        ),
        compiler_params=pltpu.CompilerParams(vmem_limit_bytes=32 * 2**20),
        name="whiten",
    )(spectra, masks)


def stack_kernel(rows_ref, own_ref, cos_ref, sin_ref, out_ref, prod_ref, even_ref, odd_ref):
    step = pl.program_id(0)
    sign = jnp.where(lax.broadcasted_iota(jnp.int32, (4, 8, 256), 1) < 4, 1.0, -1.0)
    dot = functools.partial(jnp.dot, preferred_element_type=jnp.float32)

    def one_low(f, _):
        lh, ll = halves(rows_ref[:, f].reshape(32, 128))
        left = jnp.concatenate([lh, lh, ll], axis=0).T
        for h in range(2):
            o = own_ref[:, h, f]
            q = pltpu.roll(o, 4, axis=1) * sign
            rh, rl = halves(jnp.concatenate([o.reshape(32, 256), q.reshape(32, 256)], axis=1))
            right = jnp.concatenate([rh, rl, rh], axis=0)
            prod_ref[2 * f + h] = dot(left[64 * h : 64 * h + 64], right)
        return 0

    lax.fori_loop(0, STEP, one_low, 0, unroll=True)

    @pl.when(step == 0)
    def _():
        even_ref[...] = jnp.zeros_like(even_ref)
        odd_ref[...] = jnp.zeros_like(odd_ref)

    for t in range(8):
        for part, table_ref, sum_ref in ((0, cos_ref, even_ref), (1, sin_ref, odd_ref)):
            size = sum_ref.shape[1]
            value = prod_ref[:, 8 * t : 8 * t + 8, 256 * part : 256 * part + 256].reshape(STEP * 16, 256)
            vh, vl = halves(value)
            both = dot(table_ref[0], vh)
            sum_ref[t] += both[:size] + both[size:] + dot(table_ref[0, :size], vl)

    @pl.when(step == STEPS - 1)
    def _():
        mid = LAGS // 2
        for t in range(8):
            e = even_ref[t].reshape(EVEN, 8, 256)
            o = odd_ref[t].reshape(ODD, 8, 256)
            place = pl.ds(8 * (t % 2), 8)
            out_ref[t // 2, mid, place] = e[0]
            for lag in range(1, mid + 1):
                if lag < mid:
                    out_ref[t // 2, mid + lag, place] = e[lag] - o[lag - 1]
                out_ref[t // 2, mid - lag, place] = e[lag] + o[lag - 1]


def stack(rows, own, cos_t, sin_t):
    own = own.reshape(4, 2, HALF, 8, 256)
    return pl.pallas_call(
        stack_kernel,
        grid=(STEPS,),
        in_specs=[
            pl.BlockSpec((4, STEP, 8, 128), lambda s: (0, s, 0, 0)),
            pl.BlockSpec((4, 2, STEP, 8, 256), lambda s: (0, 0, s, 0, 0)),
            pl.BlockSpec((1,) + cos_t.shape[1:], lambda s: (s, 0, 0)),
            pl.BlockSpec((1,) + sin_t.shape[1:], lambda s: (s, 0, 0)),
        ],
        out_specs=pl.BlockSpec((4, LAGS, 16, 256), lambda s: (0, 0, 0, 0)),
        scratch_shapes=[
            pltpu.VMEM((2 * STEP, 64, 512), jnp.float32),
            pltpu.VMEM((8, 8 * EVEN, 256), jnp.float32),
            pltpu.VMEM((8, 8 * ODD, 256), jnp.float32),
        ],
        out_shape=jax.ShapeDtypeStruct((4, LAGS, 16, 256), jnp.float32),
        compiler_params=pltpu.CompilerParams(vmem_limit_bytes=40 * 2**20),
        cost_estimate=pl.CostEstimate(flops=14 * 10**9, bytes_accessed=12 * 2**20, transcendentals=0),
        name="stack",
    )(rows, own, cos_t, sin_t)


def finish_kernel(first_ref, second_ref, out_ref):
    out_ref[0] = jnp.swapaxes(first_ref[...], 0, 1)
    out_ref[1] = jnp.swapaxes(second_ref[...], 0, 1)


def finish(first, second):
    return pl.pallas_call(
        finish_kernel,
        out_shape=jax.ShapeDtypeStruct((2, 16, LAGS, 256), jnp.float32),
        name="finish",
    )(first, second)


def to_partner(mask, value):
    return lax.ppermute(value, "blk", [(b, b ^ mask) for b in range(lax.axis_size("blk"))])


def by_offset(branch, offset, *values):
    count = lax.axis_size("blk")
    return lax.switch(offset - 1, [functools.partial(branch, mask) for mask in range(1, count)], *values)


def spread(value, axis):
    return lax.all_to_all(value, axis, split_axis=0, concat_axis=0, tiled=True)


def on_device(spectra, masks, plan):
    tables = [jnp.asarray(t) for t in lag_tables()]
    own, rows = whiten(spectra, masks)
    x = ("xh", "xl")
    own = lax.all_gather(own, x, axis=0, tiled=False)
    rows = spread(rows, x)
    order = lax.optimization_barrier
    theirs = by_offset(to_partner, plan[0, 0], rows)
    first = stack(theirs, own, *tables)
    first, rows = order((first, rows))
    first = lax.psum_scatter(first, "zh", scatter_dimension=0, tiled=True)[0]
    second = stack(by_offset(to_partner, plan[1, 0], rows), own, *tables)
    first, second = order((first, second))
    second = lax.psum_scatter(second, "zh", scatter_dimension=0, tiled=True)[0]
    return finish(by_offset(to_partner, plan[0, 0], first), by_offset(to_partner, plan[1, 0], second))


def solution(mesh):
    fine = Mesh(mesh.devices.reshape(16, 2, 2, 4), ("blk", "xh", "xl", "zh"))
    return jax.shard_map(
        on_device,
        mesh=fine,
        in_specs=(P(None, ("xh", "xl", "zh"), None, "blk"), P(("xh", "xl", "zh"), "blk"), P()),
        out_specs=P(None, ("blk", "xh", "xl", "zh"), None, None),
        check_vma=False,
    )
```

```python
import functools
import math

import jax
import jax.numpy as jnp
import ml_dtypes
import numpy as np
from jax import lax
from jax.experimental import pallas as pl
from jax.experimental.pallas import tpu as pltpu
from jax.sharding import Mesh
from jax.sharding import PartitionSpec as P

LAGS = 32
BINS = 192
WINDOWS = 64
HALF = BINS // 2
STEP = 16
STEPS = HALF // STEP
EVEN = 18
ODD = 16
SMEM = pl.BlockSpec(memory_space=pltpu.SMEM)


def lag_tables():
    norm = 1.0 / math.sqrt(WINDOWS * BINS)
    bins = np.arange(BINS).reshape(2, STEPS, STEP).transpose(1, 2, 0)
    tables = []
    for turn, lags in ((np.cos, np.arange(EVEN)), (np.sin, np.arange(1, ODD + 1))):
        wave = turn(np.pi * bins[..., None] * lags / BINS) * norm * (lags <= LAGS // 2)
        table = np.einsum("sfhl,jk->sljfhk", wave, np.eye(8))
        table = table.reshape(STEPS, 8 * len(lags), STEP * 2 * 8).astype(np.float32)
        high = table.astype(ml_dtypes.bfloat16)
        low = (table - high.astype(np.float32)).astype(ml_dtypes.bfloat16)
        tables.append(np.concatenate([high, low], axis=1))
    return tables


def halves(value):
    high = value.astype(jnp.bfloat16)
    return high, (value - high.astype(jnp.float32)).astype(jnp.bfloat16)


def chooser(first, second):
    common = first & second
    return jnp.where(common != 0, common & -common, (first & -first) | (second & -second))


def parity(bits):
    bits = bits ^ (bits >> 2)
    return (bits ^ (bits >> 1)) & 1


def whiten_kernel(spectra_ref, masks_ref, own_ref, rows_ref):
    parts, windows, bins, channels = spectra_ref.shape
    pieces = []
    scales = []
    for w in range(windows):
        a, b = spectra_ref[0, w], spectra_ref[1, w]
        power = jnp.sum(a * a + b * b, axis=0, keepdims=True) * (1.0 / bins)
        scales.append(masks_ref[w : w + 1, :].astype(jnp.float32) * lax.rsqrt(power + 1e-06))
    for p in range(parts):
        for w in range(windows):
            pieces.append(spectra_ref[p, w] * scales[w])
    white = jnp.swapaxes(jnp.stack(pieces, axis=0), 0, 1)
    own_ref[...] = white
    lane = lax.broadcasted_iota(jnp.int32, (HALF, 8, 128), 2)
    for block in range(channels // 128):
        a = white[:HALF, :, block * 128 : (block + 1) * 128]
        b = white[HALF:, :, block * 128 : (block + 1) * 128]
        rows_ref[2 * block] = jnp.where(lane < 64, a, pltpu.roll(b, 64, axis=2))
        rows_ref[2 * block + 1] = jnp.where(lane < 64, pltpu.roll(a, 64, axis=2), b)


def whiten(spectra, masks):
    return pl.pallas_call(
        whiten_kernel,
        out_shape=(
            jax.ShapeDtypeStruct((BINS, 8, 256), jnp.float32),
            jax.ShapeDtypeStruct((4, HALF, 8, 128), jnp.float32),
        ),
        compiler_params=pltpu.CompilerParams(vmem_limit_bytes=32 * 2**20),
        name="whiten",
    )(spectra, masks)


def stack_kernel(
    flag_ref, low_ref, high_ref, own_ref, cos_ref, sin_ref, out_ref, prod_ref, even_ref, odd_ref
):
    take_high = flag_ref[0] == 1
    step = pl.program_id(0)
    sign = jnp.where(lax.broadcasted_iota(jnp.int32, (4, 8, 256), 1) < 4, 1.0, -1.0)
    dot = functools.partial(jnp.dot, preferred_element_type=jnp.float32)

    def one_low(f, _):
        p = jnp.where(take_high, high_ref[:, f].reshape(32, 128), low_ref[:, f].reshape(32, 128))
        lh, ll = halves(p)
        left = jnp.concatenate([lh, lh, ll], axis=0).T
        for h in range(2):
            o = own_ref[:, h, f]
            q = pltpu.roll(o, 4, axis=1) * sign
            rh, rl = halves(jnp.concatenate([o.reshape(32, 256), q.reshape(32, 256)], axis=1))
            right = jnp.concatenate([rh, rl, rh], axis=0)
            prod_ref[2 * f + h] = dot(left[64 * h : 64 * h + 64], right)
        return 0

    lax.fori_loop(0, STEP, one_low, 0, unroll=True)

    @pl.when(step == 0)
    def _():
        even_ref[...] = jnp.zeros_like(even_ref)
        odd_ref[...] = jnp.zeros_like(odd_ref)

    for t in range(8):
        for part, table_ref, sum_ref in ((0, cos_ref, even_ref), (1, sin_ref, odd_ref)):
            size = sum_ref.shape[1]
            value = prod_ref[:, 8 * t : 8 * t + 8, 256 * part : 256 * part + 256].reshape(STEP * 16, 256)
            vh, vl = halves(value)
            both = dot(table_ref[0], vh)
            sum_ref[t] += both[:size] + both[size:] + dot(table_ref[0, :size], vl)

    @pl.when(step == STEPS - 1)
    def _():
        mid = LAGS // 2
        for t in range(8):
            e = even_ref[t].reshape(EVEN, 8, 256)
            o = odd_ref[t].reshape(ODD, 8, 256)
            place = pl.ds(8 * (t % 2), 8)
            out_ref[t // 2, mid, place] = e[0]
            for lag in range(1, mid + 1):
                out_ref[t // 2, mid + lag, place] = e[lag] - o[lag - 1]
                out_ref[t // 2, mid - lag, place] = e[lag] + o[lag - 1]


def stack(flag, low_rows, high_rows, own, cos_t, sin_t):
    own = own.reshape(4, 2, HALF, 8, 256)
    return pl.pallas_call(
        stack_kernel,
        grid_spec=pltpu.PrefetchScalarGridSpec(
            num_scalar_prefetch=1,
            grid=(STEPS,),
            in_specs=[pl.BlockSpec((4, STEP, 8, 128), lambda s, flag: (0, s, 0, 0))] * 2
            + [pl.BlockSpec((4, 2, STEP, 8, 256), lambda s, flag: (0, 0, s, 0, 0))]
            + [
                pl.BlockSpec((1,) + cos_t.shape[1:], lambda s, flag: (s, 0, 0)),
                pl.BlockSpec((1,) + sin_t.shape[1:], lambda s, flag: (s, 0, 0)),
            ],
            out_specs=pl.BlockSpec((4, LAGS + 1, 16, 256), lambda s, flag: (0, 0, 0, 0)),
            scratch_shapes=[
                pltpu.VMEM((2 * STEP, 64, 512), jnp.float32),
                pltpu.VMEM((8, 8 * EVEN, 256), jnp.float32),
                pltpu.VMEM((8, 8 * ODD, 256), jnp.float32),
            ],
        ),
        out_shape=jax.ShapeDtypeStruct((4, LAGS + 1, 16, 256), jnp.float32),
        compiler_params=pltpu.CompilerParams(vmem_limit_bytes=58 * 2**20),
        cost_estimate=pl.CostEstimate(flops=14 * 10**9, bytes_accessed=12 * 2**20, transcendentals=0),
        name="stack",
    )(flag, low_rows, high_rows, own, cos_t, sin_t)


def pack_kernel(sums_ref, out_ref):
    block = lax.broadcasted_iota(jnp.int32, (16, 128), 1) // 16
    for half in range(2):
        for g in range(4):
            found = [None] * 8
            for k in range(8):
                value = sums_ref[LAGS - 8 * g - k, :, 128 * half : 128 * half + 128]
                for d in range(8):
                    turned = value if d == k else pltpu.roll(value, 16 * ((k - d) % 8), axis=1)
                    found[d] = turned if k == 0 else jnp.where(block == k, turned, found[d])
            for d in range(8):
                out_ref[8 * half + d, g] = found[d]


def pack(sums):
    return pl.pallas_call(
        pack_kernel,
        out_shape=jax.ShapeDtypeStruct((16, 4, 16, 128), jnp.float32),
        cost_estimate=pl.CostEstimate(flops=10**6, bytes_accessed=2 * 2**20, transcendentals=0),
        name="pack",
    )(sums)


def finish_kernel(flags_ref, turned_ref, low_ref, high_ref, out_ref):
    own = jnp.concatenate([turned_ref[:, g].reshape(256, 128).T.reshape(8, 16, 256) for g in range(4)], axis=0)
    out_ref[flags_ref[1]] = jnp.swapaxes(own, 0, 1)
    sent = jnp.where(flags_ref[0] == 1, low_ref[:LAGS], high_ref[:LAGS])
    out_ref[1 - flags_ref[1]] = jnp.swapaxes(sent, 0, 1)


def finish(flags, turned, low, high):
    return pl.pallas_call(
        finish_kernel,
        in_specs=[SMEM] + [pl.BlockSpec(memory_space=pltpu.VMEM)] * 3,
        out_shape=jax.ShapeDtypeStruct((2, 16, LAGS, 256), jnp.float32),
        name="finish",
    )(flags, turned, low, high)


def to_partner(mask, value):
    return lax.ppermute(value, "blk", [(b, b ^ mask) for b in range(lax.axis_size("blk"))])


def by_offset(branch, offset, *values):
    count = lax.axis_size("blk")
    return lax.switch(offset - 1, [functools.partial(branch, mask) for mask in range(1, count)], *values)


def spread(value, axis):
    return lax.all_to_all(value, axis, split_axis=0, concat_axis=0, tiled=True)


def on_device(spectra, masks, plan):
    tables = [jnp.asarray(t) for t in lag_tables()]
    own, rows = whiten(spectra, masks)
    x = ("xh", "xl")
    own = lax.all_gather(own, x, axis=0, tiled=False)
    low, high = jnp.minimum(plan[0, 0], plan[1, 0]), jnp.maximum(plan[0, 0], plan[1, 0])
    flag = parity(chooser(low, high) & lax.axis_index("blk"))
    swapped = (plan[0, 0] > plan[1, 0]).astype(jnp.int32)
    order = lax.optimization_barrier
    gathered = spread(rows, x)
    theirs = by_offset(to_partner, low, rows)
    gathered, theirs = order((gathered, theirs))
    low_rows = spread(theirs, x)
    high_rows = by_offset(to_partner, high, gathered)
    sums = stack(flag[None], low_rows, high_rows, own, *tables)
    sums = lax.psum_scatter(sums, "zh", scatter_dimension=0, tiled=True)[0]
    low_back = by_offset(to_partner, low, sums)
    sums, low_back = order((sums, low_back))
    turned = spread(pack(sums), ("xh", "xl", "zh"))
    high_back = by_offset(to_partner, high, sums)
    return finish(jnp.stack([flag, flag ^ swapped]), turned, low_back, high_back)


def solution(mesh):
    fine = Mesh(mesh.devices.reshape(16, 2, 2, 4), ("blk", "xh", "xl", "zh"))
    return jax.shard_map(
        on_device,
        mesh=fine,
        in_specs=(P(None, ("xh", "xl", "zh"), None, "blk"), P(("xh", "xl", "zh"), "blk"), P()),
        out_specs=P(None, ("blk", "xh", "xl", "zh"), None, None),
        check_vma=False,
    )
```

```python
import functools
import math

import jax
import jax.numpy as jnp
import ml_dtypes
import numpy as np
from jax import lax
from jax.experimental import pallas as pl
from jax.experimental.pallas import tpu as pltpu
from jax.sharding import Mesh
from jax.sharding import PartitionSpec as P

LAGS = 32
BINS = 192
WINDOWS = 64
HALF = BINS // 2
STEP = 32
STEPS = HALF // STEP
EVEN = 18
ODD = 16
SMEM = pl.BlockSpec(memory_space=pltpu.SMEM)


def lag_tables():
    norm = 1.0 / math.sqrt(WINDOWS * BINS)
    bins = np.arange(BINS).reshape(2, STEPS, STEP).transpose(1, 2, 0)
    tables = []
    for turn, lags in ((np.cos, np.arange(EVEN)), (np.sin, np.arange(1, ODD + 1))):
        wave = turn(np.pi * bins[..., None] * lags / BINS) * norm * (lags <= LAGS // 2)
        table = np.einsum("sfhl,jk->sljfhk", wave, np.eye(8))
        table = table.reshape(STEPS, 8 * len(lags), STEP * 2 * 8).astype(np.float32)
        high = table.astype(ml_dtypes.bfloat16)
        low = (table - high.astype(np.float32)).astype(ml_dtypes.bfloat16)
        tables.append(np.concatenate([high, low], axis=1))
    return tables


def halves(value):
    high = value.astype(jnp.bfloat16)
    return high, (value - high.astype(jnp.float32)).astype(jnp.bfloat16)


def chooser(first, second):
    common = first & second
    return jnp.where(common != 0, common & -common, (first & -first) | (second & -second))


def parity(bits):
    bits = bits ^ (bits >> 2)
    return (bits ^ (bits >> 1)) & 1


def whiten_kernel(spectra_ref, masks_ref, own_ref, rows_ref):
    parts, windows, bins, channels = spectra_ref.shape
    pieces = []
    scales = []
    for w in range(windows):
        a, b = spectra_ref[0, w], spectra_ref[1, w]
        power = jnp.sum(a * a + b * b, axis=0, keepdims=True) * (1.0 / bins)
        scales.append(masks_ref[w : w + 1, :].astype(jnp.float32) * lax.rsqrt(power + 1e-06))
    for p in range(parts):
        for w in range(windows):
            pieces.append(spectra_ref[p, w] * scales[w])
    white = jnp.swapaxes(jnp.stack(pieces, axis=0), 0, 1)
    own_ref[...] = white
    lane = lax.broadcasted_iota(jnp.int32, (HALF, 8, 128), 2)
    for block in range(channels // 128):
        a = white[:HALF, :, block * 128 : (block + 1) * 128]
        b = white[HALF:, :, block * 128 : (block + 1) * 128]
        rows_ref[2 * block] = jnp.where(lane < 64, a, pltpu.roll(b, 64, axis=2))
        rows_ref[2 * block + 1] = jnp.where(lane < 64, pltpu.roll(a, 64, axis=2), b)


def whiten(spectra, masks):
    return pl.pallas_call(
        whiten_kernel,
        out_shape=(
            jax.ShapeDtypeStruct((BINS, 8, 256), jnp.float32),
            jax.ShapeDtypeStruct((4, HALF, 8, 128), jnp.float32),
        ),
        compiler_params=pltpu.CompilerParams(vmem_limit_bytes=32 * 2**20),
        name="whiten",
    )(spectra, masks)


def stack_kernel(
    flag_ref, low_ref, high_ref, own_ref, cos_ref, sin_ref, out_ref, prod_ref, even_ref, odd_ref
):
    take_high = flag_ref[0] == 1
    step = pl.program_id(0)
    sign = jnp.where(lax.broadcasted_iota(jnp.int32, (4, 8, 256), 1) < 4, 1.0, -1.0)
    dot = functools.partial(jnp.dot, preferred_element_type=jnp.float32)

    def one_low(f, _):
        p = jnp.where(take_high, high_ref[:, f].reshape(32, 128), low_ref[:, f].reshape(32, 128))
        lh, ll = halves(p)
        left = jnp.concatenate([lh, lh, ll], axis=0).T
        for h in range(2):
            o = own_ref[:, h, f]
            q = pltpu.roll(o, 4, axis=1) * sign
            rh, rl = halves(jnp.concatenate([o.reshape(32, 256), q.reshape(32, 256)], axis=1))
            right = jnp.concatenate([rh, rl, rh], axis=0)
            prod_ref[2 * f + h] = dot(left[64 * h : 64 * h + 64], right)
        return 0

    lax.fori_loop(0, STEP, one_low, 0, unroll=True)

    @pl.when(step == 0)
    def _():
        even_ref[...] = jnp.zeros_like(even_ref)
        odd_ref[...] = jnp.zeros_like(odd_ref)

    for t in range(8):
        for part, table_ref, sum_ref in ((0, cos_ref, even_ref), (1, sin_ref, odd_ref)):
            size = sum_ref.shape[1]
            value = prod_ref[:, 8 * t : 8 * t + 8, 256 * part : 256 * part + 256].reshape(STEP * 16, 256)
            vh, vl = halves(value)
            both = dot(table_ref[0], vh)
            sum_ref[t] += both[:size] + both[size:] + dot(table_ref[0, :size], vl)

    @pl.when(step == STEPS - 1)
    def _():
        mid = LAGS // 2
        for t in range(8):
            e = even_ref[t].reshape(EVEN, 8, 256)
            o = odd_ref[t].reshape(ODD, 8, 256)
            place = pl.ds(8 * (t % 2), 8)
            out_ref[t // 2, mid, place] = e[0]
            for lag in range(1, mid + 1):
                out_ref[t // 2, mid + lag, place] = e[lag] - o[lag - 1]
                out_ref[t // 2, mid - lag, place] = e[lag] + o[lag - 1]


def stack(flag, low_rows, high_rows, own, cos_t, sin_t):
    own = own.reshape(4, 2, HALF, 8, 256)
    return pl.pallas_call(
        stack_kernel,
        grid_spec=pltpu.PrefetchScalarGridSpec(
            num_scalar_prefetch=1,
            grid=(STEPS,),
            in_specs=[pl.BlockSpec((4, STEP, 8, 128), lambda s, flag: (0, s, 0, 0))] * 2
            + [pl.BlockSpec((4, 2, STEP, 8, 256), lambda s, flag: (0, 0, s, 0, 0))]
            + [
                pl.BlockSpec((1,) + cos_t.shape[1:], lambda s, flag: (s, 0, 0)),
                pl.BlockSpec((1,) + sin_t.shape[1:], lambda s, flag: (s, 0, 0)),
            ],
            out_specs=pl.BlockSpec((4, LAGS + 1, 16, 256), lambda s, flag: (0, 0, 0, 0)),
            scratch_shapes=[
                pltpu.VMEM((2 * STEP, 64, 512), jnp.float32),
                pltpu.VMEM((8, 8 * EVEN, 256), jnp.float32),
                pltpu.VMEM((8, 8 * ODD, 256), jnp.float32),
            ],
        ),
        out_shape=jax.ShapeDtypeStruct((4, LAGS + 1, 16, 256), jnp.float32),
        compiler_params=pltpu.CompilerParams(vmem_limit_bytes=58 * 2**20),
        cost_estimate=pl.CostEstimate(flops=14 * 10**9, bytes_accessed=12 * 2**20, transcendentals=0),
        name="stack",
    )(flag, low_rows, high_rows, own, cos_t, sin_t)


def pack_kernel(sums_ref, out_ref):
    block = lax.broadcasted_iota(jnp.int32, (16, 128), 1) // 16
    for half in range(2):
        for g in range(4):
            found = [None] * 8
            for k in range(8):
                value = sums_ref[LAGS - 8 * g - k, :, 128 * half : 128 * half + 128]
                for d in range(8):
                    turned = value if d == k else pltpu.roll(value, 16 * ((k - d) % 8), axis=1)
                    found[d] = turned if k == 0 else jnp.where(block == k, turned, found[d])
            for d in range(8):
                out_ref[8 * half + d, g] = found[d]


def pack(sums):
    return pl.pallas_call(
        pack_kernel,
        out_shape=jax.ShapeDtypeStruct((16, 4, 16, 128), jnp.float32),
        cost_estimate=pl.CostEstimate(flops=10**6, bytes_accessed=2 * 2**20, transcendentals=0),
        name="pack",
    )(sums)


def finish_kernel(flags_ref, turned_ref, low_ref, high_ref, out_ref):
    own = jnp.concatenate([turned_ref[:, g].reshape(256, 128).T.reshape(8, 16, 256) for g in range(4)], axis=0)
    out_ref[flags_ref[1]] = jnp.swapaxes(own, 0, 1)
    sent = jnp.where(flags_ref[0] == 1, low_ref[:LAGS], high_ref[:LAGS])
    out_ref[1 - flags_ref[1]] = jnp.swapaxes(sent, 0, 1)


def finish(flags, turned, low, high):
    return pl.pallas_call(
        finish_kernel,
        in_specs=[SMEM] + [pl.BlockSpec(memory_space=pltpu.VMEM)] * 3,
        out_shape=jax.ShapeDtypeStruct((2, 16, LAGS, 256), jnp.float32),
        name="finish",
    )(flags, turned, low, high)


def to_partner(mask, value):
    return lax.ppermute(value, "blk", [(b, b ^ mask) for b in range(lax.axis_size("blk"))])


def by_offset(branch, offset, *values):
    count = lax.axis_size("blk")
    return lax.switch(offset - 1, [functools.partial(branch, mask) for mask in range(1, count)], *values)


def spread(value, axis):
    return lax.all_to_all(value, axis, split_axis=0, concat_axis=0, tiled=True)


def on_device(spectra, masks, plan):
    tables = [jnp.asarray(t) for t in lag_tables()]
    own, rows = whiten(spectra, masks)
    x = ("xh", "xl")
    own = lax.all_gather(own, x, axis=0, tiled=False)
    low, high = jnp.minimum(plan[0, 0], plan[1, 0]), jnp.maximum(plan[0, 0], plan[1, 0])
    flag = parity(chooser(low, high) & lax.axis_index("blk"))
    swapped = (plan[0, 0] > plan[1, 0]).astype(jnp.int32)
    order = lax.optimization_barrier
    gathered = spread(rows, x)
    theirs = by_offset(to_partner, low, rows)
    gathered, theirs = order((gathered, theirs))
    low_rows = spread(theirs, x)
    high_rows = by_offset(to_partner, high, gathered)
    sums = stack(flag[None], low_rows, high_rows, own, *tables)
    sums = lax.psum_scatter(sums, "zh", scatter_dimension=0, tiled=True)[0]
    low_back = by_offset(to_partner, low, sums)
    sums, low_back = order((sums, low_back))
    turned = spread(pack(sums), ("xh", "xl", "zh"))
    high_back = by_offset(to_partner, high, sums)
    return finish(jnp.stack([flag, flag ^ swapped]), turned, low_back, high_back)


def solution(mesh):
    fine = Mesh(mesh.devices.reshape(16, 2, 2, 4), ("blk", "xh", "xl", "zh"))
    return jax.shard_map(
        on_device,
        mesh=fine,
        in_specs=(P(None, ("xh", "xl", "zh"), None, "blk"), P(("xh", "xl", "zh"), "blk"), P()),
        out_specs=P(None, ("blk", "xh", "xl", "zh"), None, None),
        check_vma=False,
    )
```

```python
import functools
import math

import jax
import jax.numpy as jnp
import ml_dtypes
import numpy as np
from jax import lax
from jax.experimental import pallas as pl
from jax.experimental.pallas import tpu as pltpu
from jax.sharding import Mesh
from jax.sharding import PartitionSpec as P

LAGS = 32
BINS = 192
WINDOWS = 64
HALF = BINS // 2
STEP = 48
STEPS = HALF // STEP
EVEN = 18
ODD = 16
SMEM = pl.BlockSpec(memory_space=pltpu.SMEM)


def lag_tables():
    norm = 1.0 / math.sqrt(WINDOWS * BINS)
    bins = np.arange(BINS).reshape(2, STEPS, STEP).transpose(1, 2, 0)
    tables = []
    for turn, lags in ((np.cos, np.arange(EVEN)), (np.sin, np.arange(1, ODD + 1))):
        wave = turn(np.pi * bins[..., None] * lags / BINS) * norm * (lags <= LAGS // 2)
        table = np.einsum("sfhl,jk->sljfhk", wave, np.eye(8))
        table = table.reshape(STEPS, 8 * len(lags), STEP * 2 * 8).astype(np.float32)
        high = table.astype(ml_dtypes.bfloat16)
        low = (table - high.astype(np.float32)).astype(ml_dtypes.bfloat16)
        tables.append(np.concatenate([high, low], axis=1))
    return tables


def halves(value):
    high = value.astype(jnp.bfloat16)
    return high, (value - high.astype(jnp.float32)).astype(jnp.bfloat16)


def chooser(first, second):
    common = first & second
    return jnp.where(common != 0, common & -common, (first & -first) | (second & -second))


def parity(bits):
    bits = bits ^ (bits >> 2)
    return (bits ^ (bits >> 1)) & 1


def whiten_kernel(spectra_ref, masks_ref, own_ref, rows_ref):
    parts, windows, bins, channels = spectra_ref.shape
    pieces = []
    scales = []
    for w in range(windows):
        a, b = spectra_ref[0, w], spectra_ref[1, w]
        power = jnp.sum(a * a + b * b, axis=0, keepdims=True) * (1.0 / bins)
        scales.append(masks_ref[w : w + 1, :].astype(jnp.float32) * lax.rsqrt(power + 1e-06))
    for p in range(parts):
        for w in range(windows):
            pieces.append(spectra_ref[p, w] * scales[w])
    white = jnp.swapaxes(jnp.stack(pieces, axis=0), 0, 1)
    own_ref[...] = white
    lane = lax.broadcasted_iota(jnp.int32, (HALF, 8, 128), 2)
    for block in range(channels // 128):
        a = white[:HALF, :, block * 128 : (block + 1) * 128]
        b = white[HALF:, :, block * 128 : (block + 1) * 128]
        rows_ref[2 * block] = jnp.where(lane < 64, a, pltpu.roll(b, 64, axis=2))
        rows_ref[2 * block + 1] = jnp.where(lane < 64, pltpu.roll(a, 64, axis=2), b)


def whiten(spectra, masks):
    return pl.pallas_call(
        whiten_kernel,
        out_shape=(
            jax.ShapeDtypeStruct((BINS, 8, 256), jnp.float32),
            jax.ShapeDtypeStruct((4, HALF, 8, 128), jnp.float32),
        ),
        compiler_params=pltpu.CompilerParams(vmem_limit_bytes=32 * 2**20),
        name="whiten",
    )(spectra, masks)


def stack_kernel(
    flag_ref, low_ref, high_ref, own_ref, cos_ref, sin_ref, out_ref, prod_ref, even_ref, odd_ref
):
    take_high = flag_ref[0] == 1
    step = pl.program_id(0)
    sign = jnp.where(lax.broadcasted_iota(jnp.int32, (4, 8, 256), 1) < 4, 1.0, -1.0)
    dot = functools.partial(jnp.dot, preferred_element_type=jnp.float32)

    def one_low(f, _):
        p = jnp.where(take_high, high_ref[:, f].reshape(32, 128), low_ref[:, f].reshape(32, 128))
        lh, ll = halves(p)
        left = jnp.concatenate([lh, lh, ll], axis=0).T
        for h in range(2):
            o = own_ref[:, h, f]
            q = pltpu.roll(o, 4, axis=1) * sign
            rh, rl = halves(jnp.concatenate([o.reshape(32, 256), q.reshape(32, 256)], axis=1))
            right = jnp.concatenate([rh, rl, rh], axis=0)
            prod_ref[2 * f + h] = dot(left[64 * h : 64 * h + 64], right)
        return 0

    lax.fori_loop(0, STEP, one_low, 0, unroll=True)

    @pl.when(step == 0)
    def _():
        even_ref[...] = jnp.zeros_like(even_ref)
        odd_ref[...] = jnp.zeros_like(odd_ref)

    for t in range(8):
        for part, table_ref, sum_ref in ((0, cos_ref, even_ref), (1, sin_ref, odd_ref)):
            size = sum_ref.shape[1]
            value = prod_ref[:, 8 * t : 8 * t + 8, 256 * part : 256 * part + 256].reshape(STEP * 16, 256)
            vh, vl = halves(value)
            both = dot(table_ref[0], vh)
            sum_ref[t] += both[:size] + both[size:] + dot(table_ref[0, :size], vl)

    @pl.when(step == STEPS - 1)
    def _():
        mid = LAGS // 2
        for t in range(8):
            e = even_ref[t].reshape(EVEN, 8, 256)
            o = odd_ref[t].reshape(ODD, 8, 256)
            place = pl.ds(8 * (t % 2), 8)
            out_ref[t // 2, mid, place] = e[0]
            for lag in range(1, mid + 1):
                out_ref[t // 2, mid + lag, place] = e[lag] - o[lag - 1]
                out_ref[t // 2, mid - lag, place] = e[lag] + o[lag - 1]


def stack(flag, low_rows, high_rows, own, cos_t, sin_t):
    own = own.reshape(4, 2, HALF, 8, 256)
    return pl.pallas_call(
        stack_kernel,
        grid_spec=pltpu.PrefetchScalarGridSpec(
            num_scalar_prefetch=1,
            grid=(STEPS,),
            in_specs=[pl.BlockSpec((4, STEP, 8, 128), lambda s, flag: (0, s, 0, 0))] * 2
            + [pl.BlockSpec((4, 2, STEP, 8, 256), lambda s, flag: (0, 0, s, 0, 0))]
            + [
                pl.BlockSpec((1,) + cos_t.shape[1:], lambda s, flag: (s, 0, 0)),
                pl.BlockSpec((1,) + sin_t.shape[1:], lambda s, flag: (s, 0, 0)),
            ],
            out_specs=pl.BlockSpec((4, LAGS + 1, 16, 256), lambda s, flag: (0, 0, 0, 0)),
            scratch_shapes=[
                pltpu.VMEM((2 * STEP, 64, 512), jnp.float32),
                pltpu.VMEM((8, 8 * EVEN, 256), jnp.float32),
                pltpu.VMEM((8, 8 * ODD, 256), jnp.float32),
            ],
        ),
        out_shape=jax.ShapeDtypeStruct((4, LAGS + 1, 16, 256), jnp.float32),
        compiler_params=pltpu.CompilerParams(vmem_limit_bytes=58 * 2**20),
        cost_estimate=pl.CostEstimate(flops=14 * 10**9, bytes_accessed=12 * 2**20, transcendentals=0),
        name="stack",
    )(flag, low_rows, high_rows, own, cos_t, sin_t)


def pack_kernel(sums_ref, out_ref):
    block = lax.broadcasted_iota(jnp.int32, (16, 128), 1) // 16
    for half in range(2):
        for g in range(4):
            found = [None] * 8
            for k in range(8):
                value = sums_ref[LAGS - 8 * g - k, :, 128 * half : 128 * half + 128]
                for d in range(8):
                    turned = value if d == k else pltpu.roll(value, 16 * ((k - d) % 8), axis=1)
                    found[d] = turned if k == 0 else jnp.where(block == k, turned, found[d])
            for d in range(8):
                out_ref[8 * half + d, g] = found[d]


def pack(sums):
    return pl.pallas_call(
        pack_kernel,
        out_shape=jax.ShapeDtypeStruct((16, 4, 16, 128), jnp.float32),
        cost_estimate=pl.CostEstimate(flops=10**6, bytes_accessed=2 * 2**20, transcendentals=0),
        name="pack",
    )(sums)


def finish_kernel(flags_ref, turned_ref, low_ref, high_ref, out_ref):
    own = jnp.concatenate([turned_ref[:, g].reshape(256, 128).T.reshape(8, 16, 256) for g in range(4)], axis=0)
    out_ref[flags_ref[1]] = jnp.swapaxes(own, 0, 1)
    sent = jnp.where(flags_ref[0] == 1, low_ref[:LAGS], high_ref[:LAGS])
    out_ref[1 - flags_ref[1]] = jnp.swapaxes(sent, 0, 1)


def finish(flags, turned, low, high):
    return pl.pallas_call(
        finish_kernel,
        in_specs=[SMEM] + [pl.BlockSpec(memory_space=pltpu.VMEM)] * 3,
        out_shape=jax.ShapeDtypeStruct((2, 16, LAGS, 256), jnp.float32),
        name="finish",
    )(flags, turned, low, high)


def to_partner(mask, value):
    return lax.ppermute(value, "blk", [(b, b ^ mask) for b in range(lax.axis_size("blk"))])


def by_offset(branch, offset, *values):
    count = lax.axis_size("blk")
    return lax.switch(offset - 1, [functools.partial(branch, mask) for mask in range(1, count)], *values)


def spread(value, axis):
    return lax.all_to_all(value, axis, split_axis=0, concat_axis=0, tiled=True)


def on_device(spectra, masks, plan):
    tables = [jnp.asarray(t) for t in lag_tables()]
    own, rows = whiten(spectra, masks)
    x = ("xh", "xl")
    own = lax.all_gather(own, x, axis=0, tiled=False)
    low, high = jnp.minimum(plan[0, 0], plan[1, 0]), jnp.maximum(plan[0, 0], plan[1, 0])
    flag = parity(chooser(low, high) & lax.axis_index("blk"))
    swapped = (plan[0, 0] > plan[1, 0]).astype(jnp.int32)
    order = lax.optimization_barrier
    gathered = spread(rows, x)
    theirs = by_offset(to_partner, low, rows)
    gathered, theirs = order((gathered, theirs))
    low_rows = spread(theirs, x)
    high_rows = by_offset(to_partner, high, gathered)
    sums = stack(flag[None], low_rows, high_rows, own, *tables)
    sums = lax.psum_scatter(sums, "zh", scatter_dimension=0, tiled=True)[0]
    low_back = by_offset(to_partner, low, sums)
    sums, low_back = order((sums, low_back))
    turned = spread(pack(sums), ("xh", "xl", "zh"))
    high_back = by_offset(to_partner, high, sums)
    return finish(jnp.stack([flag, flag ^ swapped]), turned, low_back, high_back)


def solution(mesh):
    fine = Mesh(mesh.devices.reshape(16, 2, 2, 4), ("blk", "xh", "xl", "zh"))
    return jax.shard_map(
        on_device,
        mesh=fine,
        in_specs=(P(None, ("xh", "xl", "zh"), None, "blk"), P(("xh", "xl", "zh"), "blk"), P()),
        out_specs=P(None, ("blk", "xh", "xl", "zh"), None, None),
        check_vma=False,
    )
```
